512 devices in a mesh: row: 32 (over y_hi, z), col: 16 (over y_lo, x, core).
Axes of the slice: x: 4, y: 8 (y_hi: 4, y_lo: 2; y = y_hi * 2 + y_lo), z: 8, core: 2. Of those that a mesh axis runs over, the one named last changes fastest.
Arguments:
- tiles: bfloat16 [32, 16, 96, 128, 128], P('row', 'col'), may hold values from -0.0546875 to 0.0546875
- tile_row: int32 [32, 16, 96], P('row', 'col'), may hold values from 0 to 31, as said below
- tile_col: int32 [32, 16, 96], P('row', 'col'), may hold values from 0 to 63
- tile_counts: int32 [32, 16], P('row', 'col'), may hold values from 12 to 96, as said below
- start: float32 [16, 131072], P(None, 'row'), may hold values from -16 to 16
- rotation: float32 [3, 3, 16, 16], replicated, may hold values from -3 to 3
Outputs:
- eigen_block: float32 [16, 131072], P(None, 'row')
- ritz: float32 [16, 16], replicated
The draws below stay inside these ranges and needn't reach their ends.
Inputs may be any that keep to these rules, and one draw needn't show every extreme that they name: Within a block the pairs (tile_row, tile_col) of all 96 slots are distinct. `tile_counts`: some block is full.
All inputs are finite; a program needn't handle non-finite values.
Results may differ from the reference program's by a relative error of at most 0.0003.
Values sent between devices are 32-bit elements; how exact they have to be, the bound alone decides.
No kernel may reach another device: no remote copies, remote signals or barrier semaphores. Data moves between devices by JAX's collectives and lax.ppermute only.
A program may use at most 64 MiB of HBM per device.

```python
import jax
import jax.numpy as jnp
from jax import lax

SEG = 4096
KT = 96
NV = 16
ITERS = 3
N_ROW = 32
N_COL = 16


def tile_layout(key):
    row_tiles = SEG // 128
    col_tiles = SEG * N_ROW // N_COL // 128
    keys = jax.random.split(key, N_ROW * N_COL)

    def pick_slots(sub_key):
        return jax.random.permutation(sub_key, row_tiles * col_tiles)[:KT]
    chosen = jax.vmap(pick_slots)(keys)
    return (chosen.reshape(N_ROW, N_COL, KT), col_tiles)


def draw_tile_row(key, part):
    chosen, col_tiles = tile_layout(key)
    return (chosen // col_tiles).astype(jnp.int32)


def draw_tile_col(key, part):
    chosen, col_tiles = tile_layout(key)
    return (chosen % col_tiles).astype(jnp.int32)


def draw_tile_counts(key, part):
    key = jax.random.fold_in(key, 5)
    first_key, second_key = jax.random.split(key)
    level = jax.random.randint(first_key, (N_ROW * N_COL,), 0, 8)
    counts = KT // 8 + (KT - KT // 8) * level * level // 49
    spot = jax.random.randint(second_key, (), 0, N_ROW * N_COL)
    counts = counts.at[spot].set(KT)
    return counts.reshape(N_ROW, N_COL).astype(jnp.int32)


def draw_start(key, part):
    key = jax.random.fold_in(key, 7)
    all_rows = SEG * N_ROW
    ramp = 1.0 + 2.0 * jnp.arange(all_rows, dtype=jnp.float32)[None, :] / (all_rows - 1)
    first_key = jax.random.fold_in(key, 0)
    values = jnp.clip(jax.random.normal(first_key, (NV, all_rows), jnp.float32), -4.0, 4.0) * ramp
    return values.astype(jnp.float32)


def draw_rotation(key, part):
    key = jax.random.fold_in(key, 9)
    noise = jnp.clip(jax.random.normal(key, (ITERS, 3, NV, NV), jnp.float32), -4.0, 4.0)
    weights = jnp.array([0.3, 0.6, 0.4], jnp.float32)[None, :, None, None] / jnp.sqrt(jnp.float32(NV))
    identity = jnp.eye(NV, dtype=jnp.float32)[None, None] * jnp.array([1.0, 0.0, 0.0], jnp.float32)[None, :, None, None]
    return (identity + weights * noise).astype(jnp.float32)


def shard_levels(own_key, shape, cuts, least, top_value):
    def one(position, blocks):
        steps = jax.random.uniform(jax.random.fold_in(jax.random.fold_in(own_key, 6), position), (blocks,), jnp.float32, least / len(cuts), top_value / len(cuts))
        return jnp.repeat(jnp.exp(steps), shape[position] // blocks).reshape((-1,) + (1,) * (len(shape) - position - 1))

    loudness = one(*cuts[0])
    for cut in cuts[1:]:
        loudness = loudness * one(*cut)
    return loudness


def scatter_about(key, extent, scale, bound, cuts=(), held_as=jnp.bfloat16):
    result = scale * jax.random.normal(key, extent, jnp.float32)
    if cuts:
        result = result * shard_levels(key, extent, cuts, -0.22, 0.18)
    return jnp.clip(result, -bound, bound).astype(held_as)


def setup_inputs(seed: int = 0) -> dict:
    key_of = jax.random.split(jax.random.key(seed), 7)
    return {
        "tiles": scatter_about(key_of[0], (N_ROW, N_COL, KT, 128, 128), (2 * KT * N_COL * 16384 // SEG) ** -0.5, 0.0546875, ((0, 32), (1, 16))),
        "tile_row": draw_tile_row(jax.random.fold_in(key_of[6], 71), 0),
        "tile_col": draw_tile_col(jax.random.fold_in(key_of[6], 71), 0),
        "tile_counts": draw_tile_counts(jax.random.fold_in(key_of[6], 71), 0),
        "start": draw_start(jax.random.fold_in(key_of[6], 71), 0),
        "rotation": draw_rotation(jax.random.fold_in(key_of[6], 71), 0),
    }


def apply_half(vectors, tiles, tile_row, tile_col, tile_counts):
    row_count, col_count, slot_count = tile_row.shape
    vec_count, all_rows = vectors.shape
    seg_rows = all_rows // row_count
    block_rows = all_rows // col_count
    wide = vectors.astype(jnp.float32)
    blocks = wide.reshape(vec_count, col_count, block_rows // 128, 128)
    segments = wide.reshape(vec_count, row_count, seg_rows // 128, 128)
    col_ids = jnp.arange(col_count, dtype=jnp.int32)[:, None]
    hi = lax.Precision.HIGHEST

    def one_row(running, row_index):
        tile_vals = tiles[row_index].astype(jnp.float32)
        rows_here = tile_row[row_index]
        cols_here = tile_col[row_index]
        live_slots = (jnp.arange(slot_count, dtype=jnp.int32)[None, :] < tile_counts[row_index][:, None]).astype(jnp.float32)
        picked = blocks[:, col_ids, cols_here, :]
        products = jnp.einsum('ckab,vckb->vcka', tile_vals, picked, precision=hi)
        hot_rows = (rows_here[..., None] == jnp.arange(seg_rows // 128, dtype=jnp.int32)).astype(jnp.float32) * live_slots[..., None]
        direct = jnp.einsum('vcka,ckt->vta', products, hot_rows, precision=hi).reshape(vec_count, seg_rows)
        own_seg = lax.dynamic_index_in_dim(segments, row_index, 1, keepdims=False)
        taken = own_seg[:, rows_here, :]
        mirrored = jnp.einsum('ckab,vcka->vckb', tile_vals, taken, precision=hi)
        hot_cols = (cols_here[..., None] == jnp.arange(block_rows // 128, dtype=jnp.int32)).astype(jnp.float32) * live_slots[..., None]
        spread_out = jnp.einsum('vckb,ckt->vctb', mirrored, hot_cols, precision=hi).reshape(vec_count, all_rows)
        return (running + spread_out, direct)
    mirror_total, direct_rows = lax.scan(one_row, jnp.zeros((vec_count, all_rows), jnp.float32), jnp.arange(row_count, dtype=jnp.int32))
    direct_all = jnp.transpose(direct_rows, (1, 0, 2)).reshape(vec_count, all_rows)
    return direct_all + mirror_total

def rotate(coeffs, vectors):
    return jnp.einsum('uv,un->vn', coeffs, vectors, precision=lax.Precision.HIGHEST)

def reference(tiles, tile_row, tile_col, tile_counts, start, rotation):
    hi = lax.Precision.HIGHEST
    all_rows = start.shape[1]

    def apply_op(vectors):
        return apply_half(vectors, tiles, tile_row, tile_col, tile_counts)
    current = start
    image = apply_op(current)
    search = jnp.zeros_like(start)
    search_image = jnp.zeros_like(start)
    theta = jnp.zeros((start.shape[0], start.shape[0]), jnp.float32)
    for iteration in range(ITERS):
        theta = jnp.einsum('un,vn->uv', current, image, precision=hi) / all_rows
        residual = image - rotate(theta, current)
        spread = lax.optimization_barrier(jnp.sum(residual * residual, axis=1)) / all_rows
        residual = residual / jnp.sqrt(spread + 1e-06)[:, None]
        residual_image = apply_op(residual)
        coeffs = rotation[iteration]
        new_search = rotate(coeffs[1], residual) + rotate(coeffs[2], search)
        new_search_image = rotate(coeffs[1], residual_image) + rotate(coeffs[2], search_image)
        current = rotate(coeffs[0], current) + new_search
        image = rotate(coeffs[0], image) + new_search_image
        search, search_image = (new_search, new_search_image)
    return (current, theta)
```

```python
import functools

import jax
import jax.numpy as jnp
from jax import lax
from jax.experimental import pallas as pl
from jax.experimental.pallas import tpu as pltpu
from jax.sharding import PartitionSpec as P

ITERS = 3
LANE = 128
GROUP = 8
BOTH = ("row", "col")
HIGH = lax.Precision.HIGHEST
NT = (((1,), (1,)), ((), ()))
NN = (((1,), (0,)), ((), ()))
SMEM = pl.BlockSpec(memory_space=pltpu.SMEM)
VMEM = pl.BlockSpec(memory_space=pltpu.VMEM)


def kernel_call(kernel, name, out, ins, scratch=()):
    return pl.pallas_call(
        kernel,
        name=name,
        out_shape=out,
        in_specs=ins,
        out_specs=jax.tree.map(lambda _: VMEM, out),
        scratch_shapes=scratch,
        compiler_params=pltpu.CompilerParams(vmem_limit_bytes=48 << 20),
    )


def f32(*shape):
    return jax.ShapeDtypeStruct(shape, jnp.float32)


def multiply(get_seg, get_block, count_ref, row_ref, col_ref, tiles_ref, refs, out_ref, split, total):
    seg_tiles = out_ref.shape[0]
    vecs = out_ref.shape[1]

    def keep(slot, values):
        high = values.astype(jnp.bfloat16)
        split[slot, 0:vecs, :] = high
        split[slot, vecs : 2 * vecs, :] = (values - high.astype(jnp.float32)).astype(jnp.bfloat16)

    for t in range(seg_tiles):
        keep(t, get_seg(refs, t))
        for half in range(2):
            keep(seg_tiles * (1 + half) + t, get_block(refs, t, half))
    total[...] = jnp.zeros_like(total)
    count = count_ref[0]

    def group(g, carry):
        parts = []
        for j in range(GROUP):
            slot = g * GROUP + j
            row = row_ref[slot]
            col = col_ref[slot] + seg_tiles
            tile = tiles_ref[slot]
            direct = lax.dot_general(split[col], tile, NT, preferred_element_type=jnp.float32)
            mirror = lax.dot_general(split[row], tile, NN, preferred_element_type=jnp.float32)
            live = slot < count
            parts.append((row, jnp.where(live, direct[:vecs] + direct[vecs:], 0.0)))
            parts.append((col, jnp.where(live, mirror[:vecs] + mirror[vecs:], 0.0)))
        for place, part in parts:
            total[place] += part
        return carry

    lax.fori_loop(0, (count + (GROUP - 1)) // GROUP, group, 0)
    for t in range(seg_tiles):
        out_ref[t, :, 0:LANE] = total[t]
        out_ref[t, :, LANE : 2 * LANE] = total[seg_tiles + t]
        out_ref[t, :, 2 * LANE : 3 * LANE] = total[2 * seg_tiles + t]


def multiply_first(count_ref, row_ref, col_ref, tiles_ref, seg_ref, block_ref, out_ref, split, total):
    multiply(
        lambda refs, t: refs[0][t],
        lambda refs, t, half: refs[1][t, half],
        count_ref, row_ref, col_ref, tiles_ref, (seg_ref, block_ref), out_ref, split, total,
    )


def multiply_next(count_ref, row_ref, col_ref, tiles_ref, all_ref, out_ref, split, total):
    multiply(
        lambda refs, t: refs[0][t, :, 0:LANE],
        lambda refs, t, half: refs[0][t, :, (1 + half) * LANE : (2 + half) * LANE],
        count_ref, row_ref, col_ref, tiles_ref, (all_ref,), out_ref, split, total,
    )


def add_up(got_ref, sums):
    rows, cols = got_ref.shape[0], got_ref.shape[1]
    for r in range(rows):
        half = r % 2
        sums[r // 2 : r // 2 + 1, half * LANE : (half + 1) * LANE] = jnp.sum(
            got_ref[r, :, 0:LANE], axis=0, keepdims=True
        )
    mirror = got_ref[0, :, LANE : 3 * LANE]
    for r in range(1, rows):
        mirror = mirror + got_ref[r, :, LANE : 3 * LANE]
    sums[...] = sums[...] + mirror


def sum_and_deal(got_ref, out_ref, sums):
    rows, cols = got_ref.shape[0], got_ref.shape[1]
    add_up(got_ref, sums)
    block = sums[...]
    for r in range(rows):
        half = r % 2
        out_ref[r, :, 0:LANE] = jnp.broadcast_to(
            sums[r // 2 : r // 2 + 1, half * LANE : (half + 1) * LANE], (cols, LANE)
        )
        out_ref[r, :, LANE : 3 * LANE] = block


def sum_and_deal_rows(got_ref, out_ref, sums):
    rows, cols = got_ref.shape[0], got_ref.shape[1]
    add_up(got_ref, sums)
    for r in range(rows):
        half = r % 2
        out_ref[r] = jnp.broadcast_to(
            sums[r // 2 : r // 2 + 1, half * LANE : (half + 1) * LANE], (cols, LANE)
        )


def gram(start_ref, one_ref, two_ref, three_ref, basis_ref, gram_ref):
    tiles, vecs = three_ref.shape[0], three_ref.shape[1]
    basis_ref[0:vecs, :] = start_ref[...]
    for t in range(tiles):
        lanes = slice(t * LANE, (t + 1) * LANE)
        basis_ref[vecs : 2 * vecs, lanes] = one_ref[t, :, 0:LANE]
        basis_ref[2 * vecs : 3 * vecs, lanes] = two_ref[t, :, 0:LANE]
        basis_ref[3 * vecs : 4 * vecs, lanes] = three_ref[t]
    parts = []
    for j in range(ITERS + 1):
        top = min(j + 2, ITERS + 1)
        parts.append(
            lax.dot_general(
                basis_ref[j * vecs : (j + 1) * vecs, :],
                basis_ref[j * vecs : top * vecs, :],
                NT, precision=HIGH, preferred_element_type=jnp.float32,
            )
        )
    parts.append(jnp.zeros((vecs, LANE - (2 * ITERS + 1) * vecs), jnp.float32))
    gram_ref[...] = jnp.concatenate(parts, axis=1)


def finish(states, grams_ref, turn_ref, basis_ref, eigen_ref, ritz_ref):
    vecs = eigen_ref.shape[0]

    def mul(a, b, dims=NN):
        full = jnp.concatenate([b, jnp.zeros((LANE - b.shape[0], b.shape[1]), jnp.float32)], axis=0)
        return lax.dot_general(a, full, dims, precision=HIGH, preferred_element_type=jnp.float32)

    moments = grams_ref[0]
    for r in range(1, grams_ref.shape[0]):
        moments = moments + grams_ref[r]
    moments = moments * (1.0 / states)
    hankel = jnp.concatenate(
        [moments] + [pltpu.roll(moments, LANE - j * vecs, 1) for j in range(1, ITERS)], axis=0
    )
    eye = lax.broadcasted_iota(jnp.int32, (vecs, LANE), 0) == lax.broadcasted_iota(jnp.int32, (vecs, LANE), 1)
    iterate = eye.astype(jnp.float32)
    search = None
    for i in range(ITERS):
        keep, step, past = (turn_ref[i, j] for j in range(3))
        weighted = mul(iterate, hankel) if i else moments
        own = mul(weighted, iterate, NT)
        theta = mul(pltpu.roll(weighted, LANE - vecs, 1), iterate, NT)
        images = mul(pltpu.roll(weighted, LANE - 2 * vecs, 1), iterate, NT)
        terms = jnp.where(eye, images, 0.0) - 2.0 * theta * theta + theta * mul(own, theta)
        spread = jnp.maximum(jnp.sum(terms, axis=0, keepdims=True), 0.0)
        scaled = step / jnp.sqrt(spread + 1e-06)
        residual = pltpu.roll(iterate, vecs, 1) - mul(theta, iterate)
        moved = mul(scaled, residual)
        if search is not None:
            moved = moved - mul(-past, search)
        iterate = moved - mul(-keep, iterate)
        search = moved
    ritz_ref[...] = theta[:, :vecs]
    width = 4 * LANE
    for j in range(eigen_ref.shape[1] // width):
        lanes = slice(j * width, (j + 1) * width)
        eigen_ref[:, lanes] = mul(iterate, basis_ref[:, lanes])


def body(tiles, tile_row, tile_col, tile_counts, start, rotation):
    tiles = tiles.reshape(tiles.shape[2:])
    slots = tiles.shape[0]
    vecs, seg_rows = start.shape
    rows = lax.axis_size("row")
    cols = lax.axis_size("col")
    seg_tiles = seg_rows // LANE
    index = (tile_counts.reshape(1), tile_row.reshape(slots), tile_col.reshape(slots))
    own_col = lax.axis_index("col")
    dealt = f32(seg_tiles, vecs, 3 * LANE)
    work = [
        pltpu.VMEM((3 * seg_tiles, 2 * vecs, LANE), jnp.bfloat16),
        pltpu.VMEM((3 * seg_tiles, vecs, LANE), jnp.float32),
    ]
    sums = [pltpu.VMEM((cols, 2 * LANE), jnp.float32)]
    got = f32(rows, cols, 3 * LANE)

    def swap(x):
        width = x.shape[-1]
        moved = lax.all_to_all(x.reshape(rows * cols, width), BOTH, 0, 0)
        return moved.reshape(rows, cols, width)

    start_tiles = start.reshape(vecs, seg_tiles, LANE).transpose(1, 0, 2)
    pieces = lax.all_to_all(start_tiles, "row", 0, 0)
    piece = lax.dynamic_slice_in_dim(pieces, 2 * own_col, 2, 0)
    block = lax.all_to_all(jnp.broadcast_to(piece, (rows, 2, vecs, LANE)), "row", 0, 0)

    sent = kernel_call(multiply_first, "multiply_first", dealt, [SMEM] * 3 + [VMEM] * 3, work)(
        *index, tiles, start_tiles, block
    )
    images = []
    for _ in range(ITERS - 1):
        given = kernel_call(sum_and_deal, "sum_and_deal", got, [VMEM], sums)(swap(sent))
        images.append(swap(given))
        sent = kernel_call(multiply_next, "multiply_next", dealt, [SMEM] * 3 + [VMEM] * 2, work)(
            *index, tiles, images[-1]
        )
    given = kernel_call(sum_and_deal_rows, "sum_rows", f32(rows, cols, LANE), [VMEM], sums)(swap(sent))
    images.append(swap(given))

    basis, grams = kernel_call(
        gram, "gram", (f32((ITERS + 1) * vecs, seg_rows), f32(vecs, LANE)), [VMEM] * 4
    )(start, *images)
    turned = jnp.pad(jnp.swapaxes(rotation, 2, 3), ((0, 0),) * 3 + ((0, LANE - vecs),))
    grams = lax.all_to_all(jnp.broadcast_to(grams, (rows, vecs, LANE)), "row", 0, 0)
    return kernel_call(
        functools.partial(finish, seg_rows * rows),
        "finish",
        (f32(vecs, seg_rows), f32(vecs, vecs)),
        [VMEM] * 3,
    )(grams, turned, basis)


def solution(mesh):
    return jax.shard_map(
        body,
        mesh=mesh,
        in_specs=(
            P("row", "col", None, None, None),
            P("row", "col", None),
            P("row", "col", None),
            P("row", "col"),
            P(None, "row"),
            P(),
        ),
        out_specs=(P(None, "row"), P()),
        check_vma=False,
    )
```

```python
import functools

import jax
import jax.numpy as jnp
from jax import lax
from jax.experimental import pallas as pl
from jax.experimental.pallas import tpu as pltpu
from jax.sharding import PartitionSpec as P

ITERS = 3
LANE = 128
GROUP = 8
BOTH = ("row", "col")
HIGH = lax.Precision.HIGHEST
NT = (((1,), (1,)), ((), ()))
NN = (((1,), (0,)), ((), ()))
SMEM = pl.BlockSpec(memory_space=pltpu.SMEM)
VMEM = pl.BlockSpec(memory_space=pltpu.VMEM)
ANY = pl.BlockSpec(memory_space=pl.ANY)


def kernel_call(kernel, name, out, ins, scratch=()):
    return pl.pallas_call(
        kernel,
        name=name,
        out_shape=out,
        in_specs=ins,
        out_specs=jax.tree.map(lambda _: VMEM, out),
        scratch_shapes=scratch,
        compiler_params=pltpu.CompilerParams(vmem_limit_bytes=48 << 20),
    )


def f32(*shape):
    return jax.ShapeDtypeStruct(shape, jnp.float32)


def multiply(get_seg, get_block, index, tiles_ref, refs, split, total, ready=None):
    count_ref, row_ref, col_ref = index
    seg_tiles = total.shape[0] // 3
    vecs = total.shape[1]

    def keep(slot, values):
        high = values.astype(jnp.bfloat16)
        split[slot, 0:vecs, :] = high
        split[slot, vecs : 2 * vecs, :] = (values - high.astype(jnp.float32)).astype(jnp.bfloat16)

    for t in range(seg_tiles):
        keep(t, get_seg(refs, t))
        for half in range(2):
            keep(seg_tiles * (1 + half) + t, get_block(refs, t, half))
    total[...] = jnp.zeros_like(total)
    if ready is not None:
        ready()
    count = count_ref[0]

    def group(g, carry):
        if ready is not None:
            ready(g)
        parts = []
        for j in range(GROUP):
            slot = g * GROUP + j
            row = row_ref[slot]
            col = col_ref[slot] + seg_tiles
            tile = tiles_ref[slot]
            direct = lax.dot_general(split[col], tile, NT, preferred_element_type=jnp.float32)
            mirror = lax.dot_general(split[row], tile, NN, preferred_element_type=jnp.float32)
            live = slot < count
            parts.append((row, jnp.where(live, direct[:vecs] + direct[vecs:], 0.0)))
            parts.append((col, jnp.where(live, mirror[:vecs] + mirror[vecs:], 0.0)))
        for place, part in parts:
            total[place] += part
        return carry

    groups = tiles_ref.shape[0] // GROUP if ready is not None else (count + (GROUP - 1)) // GROUP
    lax.fori_loop(0, groups, group, 0)


def lay_out(total, out_ref):
    seg_tiles = out_ref.shape[0]
    for t in range(seg_tiles):
        for part in range(3):
            out_ref[t, :, part * LANE : (part + 1) * LANE] = total[part * seg_tiles + t]


def multiply_first(count_hbm, row_hbm, col_hbm, tiles_hbm, seg_ref, block_ref, out_ref, split, total, tiles_ref, *more):
    index, index_sem, tiles_sem = more[0:3], more[3], more[4]
    seg_tiles = seg_ref.shape[0]
    vecs = seg_ref.shape[1]
    index_copies = [
        pltpu.make_async_copy(source, place, index_sem.at[i])
        for i, (source, place) in enumerate(zip((count_hbm, row_hbm, col_hbm), index))
    ]

    def tile_copy(g):
        some = pl.ds(g * GROUP, GROUP)
        return pltpu.make_async_copy(tiles_hbm.at[some], tiles_ref.at[some], tiles_sem.at[g])

    for copy in index_copies:
        copy.start()
    for g in range(tiles_ref.shape[0] // GROUP):
        tile_copy(g).start()

    def ready(g=None):
        if g is None:
            for copy in index_copies:
                copy.wait()
        else:
            tile_copy(g).wait()

    multiply(
        lambda refs, t: refs[0][t],
        lambda refs, t, half: refs[1][(half * seg_tiles + t) // 2, t % 2],
        index, tiles_ref, (seg_ref, block_ref), split, total, ready,
    )
    lay_out(total, out_ref)


def take_seg(refs, t):
    return refs[0][t, :, 0:LANE]


def take_block(refs, t, half):
    return refs[0][t, :, (1 + half) * LANE : (2 + half) * LANE]


def multiply_next(count_ref, row_ref, col_ref, tiles_ref, all_ref, out_ref, split, total):
    multiply(take_seg, take_block, (count_ref, row_ref, col_ref), tiles_ref, (all_ref,), split, total)
    lay_out(total, out_ref)


def multiply_last(count_ref, row_ref, col_ref, tiles_ref, all_ref, direct_ref, mirror_ref, split, total):
    multiply(take_seg, take_block, (count_ref, row_ref, col_ref), tiles_ref, (all_ref,), split, total)
    seg_tiles = direct_ref.shape[0]
    for t in range(seg_tiles):
        direct_ref[t] = total[t]
        for half in range(2):
            mirror_ref[half * seg_tiles + t] = total[(1 + half) * seg_tiles + t]


def add_up(got_ref, sums):
    rows, cols = got_ref.shape[0], got_ref.shape[1]
    for r in range(rows):
        half = r % 2
        sums[r // 2 : r // 2 + 1, half * LANE : (half + 1) * LANE] = jnp.sum(
            got_ref[r, :, 0:LANE], axis=0, keepdims=True
        )
    mirror = got_ref[0, :, LANE : 3 * LANE]
    for r in range(1, rows):
        mirror = mirror + got_ref[r, :, LANE : 3 * LANE]
    sums[...] = sums[...] + mirror


def sum_and_deal(got_ref, out_ref, sums):
    rows, cols = got_ref.shape[0], got_ref.shape[1]
    add_up(got_ref, sums)
    block = sums[...]
    for r in range(rows):
        half = r % 2
        out_ref[r, :, 0:LANE] = jnp.broadcast_to(
            sums[r // 2 : r // 2 + 1, half * LANE : (half + 1) * LANE], (cols, LANE)
        )
        out_ref[r, :, LANE : 3 * LANE] = block


def gram(own_ref, three_ref, gram_ref):
    vecs = three_ref.shape[1]
    basis = [jnp.concatenate([own_ref[j, i] for i in range(2)], axis=1) for j in range(ITERS)]
    basis.append(jnp.concatenate([three_ref[i] for i in range(2)], axis=1))
    parts = []
    for j in range(2 * ITERS + 1):
        parts.append(
            lax.dot_general(
                basis[j // 2], basis[(j + 1) // 2], NT, precision=HIGH, preferred_element_type=jnp.float32
            )
        )
    parts.append(jnp.zeros((vecs, LANE - (2 * ITERS + 1) * vecs), jnp.float32))
    gram_ref[...] = jnp.concatenate(parts, axis=1)


def finish(states, grams_ref, turn_ref, start_ref, one_ref, two_ref, three_ref, eigen_ref, ritz_ref):
    vecs = eigen_ref.shape[0]

    def mul(a, b, dims=NN):
        full = jnp.concatenate([b, jnp.zeros((LANE - b.shape[0], b.shape[1]), jnp.float32)], axis=0)
        return lax.dot_general(a, full, dims, precision=HIGH, preferred_element_type=jnp.float32)

    moments = grams_ref[0]
    for r in range(1, grams_ref.shape[0]):
        moments = moments + grams_ref[r]
    moments = moments * (1.0 / states)
    hankel = jnp.concatenate(
        [moments] + [pltpu.roll(moments, LANE - j * vecs, 1) for j in range(1, ITERS)], axis=0
    )
    eye = lax.broadcasted_iota(jnp.int32, (vecs, LANE), 0) == lax.broadcasted_iota(jnp.int32, (vecs, LANE), 1)
    iterate = eye.astype(jnp.float32)
    search = None
    for i in range(ITERS):
        keep, step, past = (turn_ref[i, j] for j in range(3))
        weighted = mul(iterate, hankel) if i else moments
        own = mul(weighted, iterate, NT)
        theta = mul(pltpu.roll(weighted, LANE - vecs, 1), iterate, NT)
        images = mul(pltpu.roll(weighted, LANE - 2 * vecs, 1), iterate, NT)
        terms = jnp.where(eye, images, 0.0) - 2.0 * theta * theta + theta * mul(own, theta)
        spread = jnp.maximum(jnp.sum(terms, axis=0, keepdims=True), 0.0)
        scaled = step / jnp.sqrt(spread + 1e-06)
        residual = pltpu.roll(iterate, vecs, 1) - mul(theta, iterate)
        moved = mul(scaled, residual)
        if search is not None:
            moved = moved - mul(-past, search)
        iterate = moved - mul(-keep, iterate)
        search = moved
    ritz_ref[...] = theta[:, :vecs]
    for t in range(three_ref.shape[0]):
        lanes = slice(t * LANE, (t + 1) * LANE)
        basis = [start_ref[:, lanes], one_ref[t, :, 0:LANE], two_ref[t, :, 0:LANE], three_ref[t]]
        eigen_ref[:, lanes] = mul(iterate, jnp.concatenate(basis, axis=0))


def body(tiles, tile_row, tile_col, tile_counts, start, rotation):
    tiles = tiles.reshape(tiles.shape[2:])
    slots = tiles.shape[0]
    vecs, seg_rows = start.shape
    rows = lax.axis_size("row")
    cols = lax.axis_size("col")
    seg_tiles = seg_rows // LANE
    index = (tile_counts.reshape(1), tile_row.reshape(slots), tile_col.reshape(slots))
    own_col = lax.axis_index("col")
    dealt = f32(seg_tiles, vecs, 3 * LANE)
    work = [
        pltpu.VMEM((3 * seg_tiles, 2 * vecs, LANE), jnp.bfloat16),
        pltpu.VMEM((3 * seg_tiles, vecs, LANE), jnp.float32),
    ]
    fetched = [
        pltpu.VMEM(tiles.shape, tiles.dtype),
        pltpu.SMEM((1,), jnp.int32),
        pltpu.SMEM((slots,), jnp.int32),
        pltpu.SMEM((slots,), jnp.int32),
        pltpu.SemaphoreType.DMA((3,)),
        pltpu.SemaphoreType.DMA((slots // GROUP,)),
    ]
    sums = [pltpu.VMEM((cols, 2 * LANE), jnp.float32)]
    got = f32(rows, cols, 3 * LANE)
    corner = []
    for r in range(rows):
        for c in range(cols):
            corner.append((r * cols + c, ((r % 2) * cols + c) * cols + r // 2))

    def swap(x):
        width = x.shape[-1]
        moved = lax.all_to_all(x.reshape(rows * cols, width), BOTH, 0, 0)
        return moved.reshape(rows, cols, width)

    def own_tiles(x):
        return lax.dynamic_slice_in_dim(x, 2 * own_col, 2, 0)[:, :, :LANE]

    start_tiles = start.reshape(vecs, seg_tiles, LANE).transpose(1, 0, 2)
    own_start = own_tiles(start_tiles)
    piece = lax.ppermute(own_start, BOTH, corner)
    block = lax.all_to_all(jnp.broadcast_to(piece, (rows, 2, vecs, LANE)), "row", 0, 0)

    sent = kernel_call(multiply_first, "multiply_first", dealt, [ANY] * 4 + [VMEM] * 2, work + fetched)(
        *index, tiles, start_tiles, block
    )
    images = []
    for i in range(ITERS - 1):
        given = kernel_call(sum_and_deal, "sum_and_deal", got, [VMEM], sums)(swap(sent))
        images.append(swap(given))
        if i < ITERS - 2:
            sent = kernel_call(multiply_next, "multiply_next", dealt, [SMEM] * 3 + [VMEM] * 2, work)(
                *index, tiles, images[-1]
            )
    direct, mirror = kernel_call(
        multiply_last,
        "multiply_last",
        (f32(seg_tiles, vecs, LANE), f32(2 * seg_tiles, vecs, LANE)),
        [SMEM] * 3 + [VMEM] * 2,
        work,
    )(*index, tiles, images[-1])

    mirror = jnp.sum(lax.all_to_all(mirror.reshape(rows, 2, vecs, LANE), "row", 0, 0), axis=0)
    direct, mirror = lax.optimization_barrier((direct, mirror))
    turned_back = lax.ppermute(mirror, BOTH, [(to, at) for at, to in corner])
    direct = jnp.sum(lax.all_to_all(direct.reshape(cols, 2, vecs, LANE), "col", 0, 0), axis=0)
    last_piece = direct + turned_back
    own = jnp.stack([own_start] + [own_tiles(image) for image in images])
    grams = kernel_call(gram, "gram", f32(vecs, LANE), [VMEM] * 2)(own, last_piece)
    shared = jnp.concatenate([last_piece, grams[None]], axis=0)
    shared = lax.all_to_all(jnp.broadcast_to(shared, (cols, 3, vecs, LANE)), "col", 0, 0)
    last = shared[:, 0:2].reshape(seg_tiles, vecs, LANE)
    grams = jnp.sum(shared[:, 2], axis=0)
    grams = lax.all_to_all(jnp.broadcast_to(grams, (rows, vecs, LANE)), "row", 0, 0)
    turned = jnp.pad(jnp.swapaxes(rotation, 2, 3), ((0, 0),) * 3 + ((0, LANE - vecs),))
    return kernel_call(
        functools.partial(finish, seg_rows * rows),
        "finish",
        (f32(vecs, seg_rows), f32(vecs, vecs)),
        [VMEM] * 6,
    )(grams, turned, start, *images, last)


def solution(mesh):
    return jax.shard_map(
        body,
        mesh=mesh,
        in_specs=(
            P("row", "col", None, None, None),
            P("row", "col", None),
            P("row", "col", None),
            P("row", "col"),
            P(None, "row"),
            P(),
        ),
        out_specs=(P(None, "row"), P()),
        check_vma=False,
    )
```

```python
import functools

import jax
import jax.numpy as jnp
from jax import lax
from jax.experimental import pallas as pl
from jax.experimental.pallas import tpu as pltpu
from jax.sharding import PartitionSpec as P

ITERS = 3
LANE = 128
GROUP = 8
BOTH = ("row", "col")
HIGH = lax.Precision.HIGHEST
NT = (((1,), (1,)), ((), ()))
NN = (((1,), (0,)), ((), ()))
SMEM = pl.BlockSpec(memory_space=pltpu.SMEM)
VMEM = pl.BlockSpec(memory_space=pltpu.VMEM)


def kernel_call(kernel, name, out, ins, scratch=()):
    return pl.pallas_call(
        kernel,
        name=name,
        out_shape=out,
        in_specs=ins,
        out_specs=jax.tree.map(lambda _: VMEM, out),
        scratch_shapes=scratch,
        compiler_params=pltpu.CompilerParams(vmem_limit_bytes=48 << 20),
    )


def f32(*shape):
    return jax.ShapeDtypeStruct(shape, jnp.float32)


def multiply(get_seg, get_block, index_ref, tiles_ref, refs, split, total):
    seg_tiles = total.shape[0] // 3
    vecs = total.shape[1]

    def keep(slot, values):
        high = values.astype(jnp.bfloat16)
        split[slot, 0:vecs, :] = high
        split[slot, vecs : 2 * vecs, :] = (values - high.astype(jnp.float32)).astype(jnp.bfloat16)

    for t in range(seg_tiles):
        keep(t, get_seg(refs, t))
        for half in range(2):
            keep(seg_tiles * (1 + half) + t, get_block(refs, t, half))
    total[...] = jnp.zeros_like(total)
    slots = tiles_ref.shape[0]
    count = index_ref[2 * slots]

    def group(g, carry):
        parts = []
        for j in range(GROUP):
            slot = g * GROUP + j
            row = index_ref[slot]
            col = index_ref[slots + slot] + seg_tiles
            tile = tiles_ref[slot]
            direct = lax.dot_general(split[col], tile, NT, preferred_element_type=jnp.float32)
            mirror = lax.dot_general(split[row], tile, NN, preferred_element_type=jnp.float32)
            live = slot < count
            parts.append((row, jnp.where(live, direct[:vecs] + direct[vecs:], 0.0)))
            parts.append((col, jnp.where(live, mirror[:vecs] + mirror[vecs:], 0.0)))
        for place, part in parts:
            total[place] += part
        return carry

    lax.fori_loop(0, (count + (GROUP - 1)) // GROUP, group, 0)


def line(t, vecs, part):
    return pl.ds(t * vecs * 3 + part, vecs, stride=3)


def lay_out(total, out_ref):
    seg_tiles, vecs = total.shape[0] // 3, total.shape[1]
    for t in range(seg_tiles):
        for part in range(3):
            out_ref[line(t, vecs, part), :] = total[part * seg_tiles + t]


def multiply_first(index_ref, tiles_ref, seg_ref, block_ref, out_ref, split, total):
    seg_tiles = seg_ref.shape[1] // LANE
    multiply(
        lambda refs, t: refs[0][:, t * LANE : (t + 1) * LANE],
        lambda refs, t, half: refs[1][(half * seg_tiles + t) // 2, :, (t % 2) * LANE : (t % 2 + 1) * LANE],
        index_ref, tiles_ref, (seg_ref, block_ref), split, total,
    )
    lay_out(total, out_ref)


def multiply_next(index_ref, tiles_ref, all_ref, out_ref, split, total):
    vecs = total.shape[1]
    multiply(
        lambda refs, t: refs[0][line(t, vecs, 0), :],
        lambda refs, t, half: refs[0][line(t, vecs, 1 + half), :],
        index_ref, tiles_ref, (all_ref,), split, total,
    )
    lay_out(total, out_ref)


def multiply_last(index_ref, tiles_ref, all_ref, direct_ref, mirror_ref, split, total):
    vecs = total.shape[1]
    multiply(
        lambda refs, t: refs[0][line(t, vecs, 0), :],
        lambda refs, t, half: refs[0][line(t, vecs, 1 + half), :],
        index_ref, tiles_ref, (all_ref,), split, total,
    )
    for refs, base in ((direct_ref, 0), (mirror_ref, total.shape[0] // 3)):
        for t in range(2 * refs.shape[0]):
            refs[t // 2, :, (t % 2) * LANE : (t % 2 + 1) * LANE] = total[base + t]


def sum_and_deal(rows, cols, got_ref, out_ref, sums):
    for r in range(rows):
        half = r % 2
        sums[r // 2 : r // 2 + 1, half * LANE : (half + 1) * LANE] = jnp.sum(
            got_ref[line(r, cols, 0), :], axis=0, keepdims=True
        )
    for half in range(2):
        mirror = got_ref[line(0, cols, 1 + half), :]
        for r in range(1, rows):
            mirror = mirror + got_ref[line(r, cols, 1 + half), :]
        lanes = slice(half * LANE, (half + 1) * LANE)
        sums[:, lanes] = sums[:, lanes] + mirror
    for r in range(rows):
        half = r % 2
        out_ref[line(r, cols, 0), :] = jnp.broadcast_to(
            sums[r // 2 : r // 2 + 1, half * LANE : (half + 1) * LANE], (cols, LANE)
        )
        for half in range(2):
            out_ref[line(r, cols, 1 + half), :] = sums[:, half * LANE : (half + 1) * LANE]


def gram(own_ref, three_ref, gram_ref):
    vecs = three_ref.shape[0]
    basis = [own_ref[j] for j in range(ITERS)] + [three_ref[...]]
    parts = []
    for j in range(2 * ITERS + 1):
        parts.append(
            lax.dot_general(
                basis[j // 2], basis[(j + 1) // 2], NT, precision=HIGH, preferred_element_type=jnp.float32
            )
        )
    parts.append(jnp.zeros((vecs, LANE - (2 * ITERS + 1) * vecs), jnp.float32))
    gram_ref[...] = jnp.concatenate(parts, axis=1)


def finish(states, grams_ref, turn_ref, start_ref, one_ref, two_ref, three_ref, eigen_ref, ritz_ref):
    vecs = eigen_ref.shape[0]

    def mul(a, b, dims=NN):
        full = jnp.concatenate([b, jnp.zeros((LANE - b.shape[0], b.shape[1]), jnp.float32)], axis=0)
        return lax.dot_general(a, full, dims, precision=HIGH, preferred_element_type=jnp.float32)

    moments = grams_ref[0]
    for r in range(1, grams_ref.shape[0]):
        moments = moments + grams_ref[r]
    moments = moments * (1.0 / states)
    hankel = jnp.concatenate(
        [moments] + [pltpu.roll(moments, LANE - j * vecs, 1) for j in range(1, ITERS)], axis=0
    )
    eye = lax.broadcasted_iota(jnp.int32, (vecs, LANE), 0) == lax.broadcasted_iota(jnp.int32, (vecs, LANE), 1)
    iterate = eye.astype(jnp.float32)
    search = None
    for i in range(ITERS):
        keep, step, past = (turn_ref[i, j] for j in range(3))
        weighted = mul(iterate, hankel) if i else moments
        own = mul(weighted, iterate, NT)
        theta = mul(pltpu.roll(weighted, LANE - vecs, 1), iterate, NT)
        images = mul(pltpu.roll(weighted, LANE - 2 * vecs, 1), iterate, NT)
        terms = jnp.where(eye, images, 0.0) - 2.0 * theta * theta + theta * mul(own, theta)
        spread = jnp.maximum(jnp.sum(terms, axis=0, keepdims=True), 0.0)
        scaled = step / jnp.sqrt(spread + 1e-06)
        residual = pltpu.roll(iterate, vecs, 1) - mul(theta, iterate)
        moved = mul(scaled, residual)
        if search is not None:
            moved = moved - mul(-past, search)
        iterate = moved - mul(-keep, iterate)
        search = moved
    ritz_ref[...] = theta[:, :vecs]
    for t in range(eigen_ref.shape[1] // LANE):
        lanes = slice(t * LANE, (t + 1) * LANE)
        own = slice((t % 2) * LANE, (t % 2 + 1) * LANE)
        basis = [start_ref[:, lanes], one_ref[line(t, vecs, 0), :], two_ref[line(t, vecs, 0), :]]
        basis.append(three_ref[t // 2, :, own])
        eigen_ref[:, lanes] = mul(iterate, jnp.concatenate(basis, axis=0))


def body(tiles, tile_row, tile_col, tile_counts, start, rotation):
    tiles = tiles.reshape(tiles.shape[2:])
    slots = tiles.shape[0]
    vecs, seg_rows = start.shape
    rows = lax.axis_size("row")
    cols = lax.axis_size("col")
    seg_tiles = seg_rows // LANE
    pair = 2 * LANE
    index = jnp.concatenate([tile_row.reshape(slots), tile_col.reshape(slots), tile_counts.reshape(1)])
    own_col = lax.axis_index("col")
    dealt = f32(rows * cols * 3, LANE)
    work = [
        pltpu.VMEM((3 * seg_tiles, 2 * vecs, LANE), jnp.bfloat16),
        pltpu.VMEM((3 * seg_tiles, vecs, LANE), jnp.float32),
    ]
    sums = [pltpu.VMEM((cols, pair), jnp.float32)]
    corner = []
    for r in range(rows):
        for c in range(cols):
            corner.append((r * cols + c, ((r % 2) * cols + c) * cols + r // 2))

    def swap(x):
        moved = lax.all_to_all(x.reshape(rows * cols, 3 * LANE), BOTH, 0, 0)
        return moved.reshape(rows * cols * 3, LANE)

    def own_tiles(x):
        x = lax.dynamic_slice_in_dim(x, own_col * (2 * vecs * 3), 2 * vecs * 3, 0).reshape(2, vecs, 3, LANE)
        return jnp.concatenate([x[0, :, 0], x[1, :, 0]], axis=1)

    def to_all(x, axis):
        count = lax.axis_size(axis)
        return lax.all_to_all(jnp.broadcast_to(x, (count,) + x.shape), axis, 0, 0)

    own_start = lax.dynamic_slice_in_dim(start, own_col * pair, pair, 1)
    index, piece = lax.optimization_barrier((index, lax.ppermute(own_start, BOTH, corner)))
    block = to_all(piece, "row")
    sent = kernel_call(multiply_first, "multiply_first", dealt, [SMEM] + [VMEM] * 3, work)(
        index, tiles, start, block
    )
    images = []
    for i in range(ITERS - 1):
        add = functools.partial(sum_and_deal, rows, cols)
        images.append(swap(kernel_call(add, "sum_and_deal", dealt, [VMEM], sums)(swap(sent))))
        if i < ITERS - 2:
            sent = kernel_call(multiply_next, "multiply_next", dealt, [SMEM] + [VMEM] * 2, work)(
                index, tiles, images[-1]
            )
    direct, mirror = kernel_call(
        multiply_last,
        "multiply_last",
        (f32(cols, vecs, pair), f32(rows, vecs, pair)),
        [SMEM] + [VMEM] * 2,
        work,
    )(index, tiles, images[-1])

    mirror = jnp.sum(lax.all_to_all(mirror, "row", 0, 0), axis=0)
    direct, mirror = lax.optimization_barrier((direct, mirror))
    turned_back = lax.ppermute(mirror, BOTH, [(to, at) for at, to in corner])
    last_piece = jnp.sum(lax.all_to_all(direct, "col", 0, 0), axis=0) + turned_back
    own = jnp.stack([own_start] + [own_tiles(image) for image in images])
    grams = kernel_call(gram, "gram", f32(vecs, LANE), [VMEM] * 2)(own, last_piece)
    grams = jnp.sum(to_all(grams, "row"), axis=0)
    last, grams = lax.optimization_barrier((lax.all_gather(last_piece, "col"), grams))
    grams = to_all(grams, "col")
    turned = jnp.pad(jnp.swapaxes(rotation, 2, 3), ((0, 0),) * 3 + ((0, LANE - vecs),))
    return kernel_call(
        functools.partial(finish, seg_rows * rows),
        "finish",
        (f32(vecs, seg_rows), f32(vecs, vecs)),
        [VMEM] * 6,
    )(grams, turned, start, *images, last)


def solution(mesh):
    return jax.shard_map(
        body,
        mesh=mesh,
        in_specs=(
            P("row", "col", None, None, None),
            P("row", "col", None),
            P("row", "col", None),
            P("row", "col"),
            P(None, "row"),
            P(),
        ),
        out_specs=(P(None, "row"), P()),
        check_vma=False,
    )
```

```python
import functools

import jax
import jax.numpy as jnp
from jax import lax
from jax.experimental import pallas as pl
from jax.experimental.pallas import tpu as pltpu
from jax.sharding import PartitionSpec as P

ITERS = 3
LANE = 128
GROUP = 32
BOTH = ("row", "col")
HIGH = lax.Precision.HIGHEST
NT = (((1,), (1,)), ((), ()))
NN = (((1,), (0,)), ((), ()))
SMEM = pl.BlockSpec(memory_space=pltpu.SMEM)
VMEM = pl.BlockSpec(memory_space=pltpu.VMEM)


def kernel_call(kernel, name, out, ins, scratch=()):
    return pl.pallas_call(
        kernel,
        name=name,
        out_shape=out,
        in_specs=ins,
        out_specs=jax.tree.map(lambda _: VMEM, out),
        scratch_shapes=scratch,
        compiler_params=pltpu.CompilerParams(vmem_limit_bytes=16 << 20),
    )


def f32(*shape):
    return jax.ShapeDtypeStruct(shape, jnp.float32)


def line(t, vecs, part):
    return pl.ds(t * vecs * 3 + part, vecs, stride=3)


def keep(split, slot, values):
    vecs = values.shape[0]
    high = values.astype(jnp.bfloat16)
    split[slot, 0:vecs, :] = high
    split[slot, vecs : 2 * vecs, :] = (values - high.astype(jnp.float32)).astype(jnp.bfloat16)


def multiply(index_ref, tiles_ref, split, total, direct, mirror):
    seg_tiles = total.shape[0] // 3
    vecs = total.shape[1]
    slots = tiles_ref.shape[0]
    count = index_ref[2 * slots]
    size = GROUP if slots % GROUP == 0 else slots
    total[...] = jnp.zeros_like(total)

    def group(g, carry):
        parts = []
        for j in range(size):
            slot = g * size + j
            row = index_ref[slot]
            col = index_ref[slots + slot] + seg_tiles
            tile = tiles_ref[slot]
            live = slot < count
            for wanted, taken, place, dims in ((direct, col, row, NT), (mirror, row, col, NN)):
                if wanted:
                    part = lax.dot_general(split[taken], tile, dims, preferred_element_type=jnp.float32)
                    parts.append((place, jnp.where(live, part[:vecs] + part[vecs:], 0.0)))
        for place, part in parts:
            total[place] += part
        return carry

    lax.fori_loop(0, (count + (size - 1)) // size, group, 0)


def first_mirror(index_ref, tiles_ref, seg_ref, out_ref, split, total):
    seg_tiles = total.shape[0] // 3
    for t in range(seg_tiles):
        keep(split, t, seg_ref[:, t * LANE : (t + 1) * LANE])
    multiply(index_ref, tiles_ref, split, total, False, True)
    out_ref[...] = total[seg_tiles : 3 * seg_tiles]


def first_direct(index_ref, tiles_ref, block_ref, mirrored_ref, out_ref, split, total):
    seg_tiles, vecs = total.shape[0] // 3, total.shape[1]
    for t in range(2 * seg_tiles):
        keep(split, seg_tiles + t, block_ref[t // 2, :, (t % 2) * LANE : (t % 2 + 1) * LANE])
    multiply(index_ref, tiles_ref, split, total, True, False)
    for t in range(seg_tiles):
        out_ref[line(t, vecs, 0), :] = total[t]
        for half in range(2):
            out_ref[line(t, vecs, 1 + half), :] = mirrored_ref[half * seg_tiles + t]


def multiply_next(index_ref, tiles_ref, all_ref, out_ref, split, total):
    seg_tiles, vecs = total.shape[0] // 3, total.shape[1]
    for t in range(seg_tiles):
        for part in range(3):
            keep(split, part * seg_tiles + t, all_ref[line(t, vecs, part), :])
    multiply(index_ref, tiles_ref, split, total, True, True)
    for t in range(seg_tiles):
        for part in range(3):
            out_ref[line(t, vecs, part), :] = total[part * seg_tiles + t]


def add_up(rows, cols, got_ref, sums):
    for r in range(rows):
        half = r % 2
        sums[r // 2 : r // 2 + 1, half * LANE : (half + 1) * LANE] = jnp.sum(
            got_ref[line(r, cols, 0), :], axis=0, keepdims=True
        )
    for half in range(2):
        mirror = got_ref[line(0, cols, 1 + half), :]
        for r in range(1, rows):
            mirror = mirror + got_ref[line(r, cols, 1 + half), :]
        lanes = slice(half * LANE, (half + 1) * LANE)
        sums[:, lanes] = sums[:, lanes] + mirror


def sum_and_deal(rows, cols, got_ref, out_ref, own_ref, sums):
    add_up(rows, cols, got_ref, sums)
    for half in range(2):
        own_ref[pl.ds(half, cols, stride=2), :] = sums[:, half * LANE : (half + 1) * LANE]
    for r in range(rows):
        half = r % 2
        out_ref[line(r, cols, 0), :] = jnp.broadcast_to(
            sums[r // 2 : r // 2 + 1, half * LANE : (half + 1) * LANE], (cols, LANE)
        )
        for half in range(2):
            out_ref[line(r, cols, 1 + half), :] = sums[:, half * LANE : (half + 1) * LANE]


def sum_and_show(rows, cols, got_ref, two_ref, out_ref, sums):
    add_up(rows, cols, got_ref, sums)
    for c in range(cols):
        out_ref[c, 0:rows, :] = two_ref[...]
        for half in range(2):
            out_ref[c, pl.ds(rows + half, cols, stride=2), :] = sums[:, half * LANE : (half + 1) * LANE]


def dots(a, b):
    return lax.dot_general(a, b, NT, precision=HIGH, preferred_element_type=jnp.float32)


def gram_known(start_ref, one_ref, two_ref, gram_ref, basis):
    vecs = start_ref.shape[0]
    for t in range(start_ref.shape[1] // LANE):
        lanes = slice(t * LANE, (t + 1) * LANE)
        basis[0:vecs, lanes] = one_ref[line(t, vecs, 0), :]
        basis[vecs : 2 * vecs, lanes] = two_ref[line(t, vecs, 0), :]
    held = [start_ref[...], basis[0:vecs, :], basis[vecs : 2 * vecs, :]]
    parts = [dots(held[j // 2], held[(j + 1) // 2]) for j in range(2 * ITERS - 1)]
    parts.append(jnp.zeros((vecs, LANE - (2 * ITERS - 1) * vecs), jnp.float32))
    gram_ref[...] = jnp.concatenate(parts, axis=1)


def gram_last(rows, known_ref, shown_ref, out_ref, basis):
    vecs = known_ref.shape[0]
    for s in range(rows):
        lanes = slice(s * LANE, (s + 1) * LANE)
        basis[0:vecs, lanes] = shown_ref[pl.ds(s, vecs, stride=2 * rows), :]
        three = shown_ref[pl.ds(rows + s, vecs, stride=2 * rows), :]
        basis[vecs : 2 * vecs, lanes] = three
        out_ref[s, 0] = three
    two, three = basis[0:vecs, :], basis[vecs : 2 * vecs, :]
    width = (2 * ITERS - 1) * vecs
    parts = [known_ref[...][:, :width], dots(two, three), dots(three, three)]
    parts.append(jnp.zeros((vecs, LANE - (2 * ITERS + 1) * vecs), jnp.float32))
    grams = jnp.concatenate(parts, axis=1)
    for s in range(rows):
        out_ref[s, 1] = grams


def finish(states, last_ref, turn_ref, start_ref, one_ref, two_ref, eigen_ref, ritz_ref):
    vecs = eigen_ref.shape[0]

    def mul(a, b, dims=NN):
        full = jnp.concatenate([b, jnp.zeros((LANE - b.shape[0], b.shape[1]), jnp.float32)], axis=0)
        return lax.dot_general(a, full, dims, precision=HIGH, preferred_element_type=jnp.float32)

    moments = last_ref[0, 1]
    for r in range(1, last_ref.shape[0]):
        moments = moments + last_ref[r, 1]
    moments = moments * (1.0 / states)
    hankel = jnp.concatenate(
        [moments] + [pltpu.roll(moments, LANE - j * vecs, 1) for j in range(1, ITERS)], axis=0
    )
    eye = lax.broadcasted_iota(jnp.int32, (vecs, LANE), 0) == lax.broadcasted_iota(jnp.int32, (vecs, LANE), 1)
    iterate = eye.astype(jnp.float32)
    search = None
    for i in range(ITERS):
        keep_turn, step, past = (turn_ref[i, j] for j in range(3))
        weighted = mul(iterate, hankel) if i else moments
        own = mul(weighted, iterate, NT)
        theta = mul(pltpu.roll(weighted, LANE - vecs, 1), iterate, NT)
        images = mul(pltpu.roll(weighted, LANE - 2 * vecs, 1), iterate, NT)
        terms = jnp.where(eye, images, 0.0) - 2.0 * theta * theta + theta * mul(own, theta)
        spread = jnp.maximum(jnp.sum(terms, axis=0, keepdims=True), 0.0)
        scaled = step / jnp.sqrt(spread + 1e-06)
        residual = pltpu.roll(iterate, vecs, 1) - mul(theta, iterate)
        moved = mul(scaled, residual)
        if search is not None:
            moved = moved - mul(-past, search)
        iterate = moved - mul(-keep_turn, iterate)
        search = moved
    ritz_ref[...] = theta[:, :vecs]
    for t in range(eigen_ref.shape[1] // LANE):
        lanes = slice(t * LANE, (t + 1) * LANE)
        basis = [start_ref[:, lanes], one_ref[line(t, vecs, 0), :], two_ref[line(t, vecs, 0), :], last_ref[t, 0]]
        eigen_ref[:, lanes] = mul(iterate, jnp.concatenate(basis, axis=0))


def body(tiles, tile_row, tile_col, tile_counts, start, rotation):
    tiles = tiles.reshape(tiles.shape[2:])
    slots = tiles.shape[0]
    vecs, seg_rows = start.shape
    rows = lax.axis_size("row")
    cols = lax.axis_size("col")
    seg_tiles = seg_rows // LANE
    pair = 2 * LANE
    index = jnp.concatenate([tile_row.reshape(slots), tile_col.reshape(slots), tile_counts.reshape(1)])
    own_col = lax.axis_index("col")
    dealt = f32(rows * cols * 3, LANE)
    work = [
        pltpu.VMEM((3 * seg_tiles, 2 * vecs, LANE), jnp.bfloat16),
        pltpu.VMEM((3 * seg_tiles, vecs, LANE), jnp.float32),
    ]
    sums = [pltpu.VMEM((cols, pair), jnp.float32)]
    basis = [pltpu.VMEM((2 * vecs, seg_rows), jnp.float32)]
    corner = []
    for r in range(rows):
        for c in range(cols):
            corner.append((r * cols + c, ((r % 2) * cols + c) * cols + r // 2))

    def swap(x):
        moved = lax.all_to_all(x.reshape(rows * cols, 3 * LANE), BOTH, 0, 0)
        return moved.reshape(rows * cols * 3, LANE)

    own_start = lax.dynamic_slice_in_dim(start, own_col * pair, pair, 1)
    index, piece = lax.optimization_barrier((index, lax.ppermute(own_start, BOTH, corner)))
    block = lax.all_to_all(jnp.broadcast_to(piece, (rows, vecs, pair)), "row", 0, 0)
    mirrored = kernel_call(
        first_mirror, "first_mirror", f32(2 * seg_tiles, vecs, LANE), [SMEM] + [VMEM] * 2, work
    )(index, tiles, start)
    sent = kernel_call(first_direct, "first_direct", dealt, [SMEM] + [VMEM] * 3, work)(
        index, tiles, block, mirrored
    )
    images = []
    for _ in range(ITERS - 1):
        given, own = kernel_call(
            functools.partial(sum_and_deal, rows, cols), "sum_and_deal", (dealt, f32(rows, LANE)), [VMEM], sums
        )(swap(sent))
        images.append(swap(given))
        sent = kernel_call(multiply_next, "multiply_next", dealt, [SMEM] + [VMEM] * 2, work)(
            index, tiles, images[-1]
        )
    shown = kernel_call(
        functools.partial(sum_and_show, rows, cols), "sum_and_show", f32(cols, 2 * rows, LANE), [VMEM] * 2, sums
    )(swap(sent), own)
    shown = lax.all_to_all(shown, "col", 0, 0).reshape(cols * 2 * rows, LANE)
    known = kernel_call(gram_known, "gram_known", f32(vecs, LANE), [VMEM] * 3, basis)(start, *images)
    last = kernel_call(
        functools.partial(gram_last, rows), "gram_last", f32(rows, 2, vecs, LANE), [VMEM] * 2, basis
    )(known, shown)
    last = lax.all_to_all(last, "row", 0, 0)
    turned = jnp.pad(jnp.swapaxes(rotation, 2, 3), ((0, 0),) * 3 + ((0, LANE - vecs),))
    return kernel_call(
        functools.partial(finish, seg_rows * rows), "finish", (f32(vecs, seg_rows), f32(vecs, vecs)), [VMEM] * 5
    )(last, turned, start, *images)


def solution(mesh):
    return jax.shard_map(
        body,
        mesh=mesh,
        in_specs=(
            P("row", "col", None, None, None),
            P("row", "col", None),
            P("row", "col", None),
            P("row", "col"),
            P(None, "row"),
            P(),
        ),
        out_specs=(P(None, "row"), P()),
        check_vma=False,
    )
```

```python
import functools

import jax
import jax.numpy as jnp
from jax import lax
from jax.experimental import pallas as pl
from jax.experimental.pallas import tpu as pltpu
from jax.sharding import PartitionSpec as P

ITERS = 3
LANE = 128
GROUP = 32
BOTH = ("row", "col")
HIGH = lax.Precision.HIGHEST
NT = (((1,), (1,)), ((), ()))
NN = (((1,), (0,)), ((), ()))
SMEM = pl.BlockSpec(memory_space=pltpu.SMEM)
VMEM = pl.BlockSpec(memory_space=pltpu.VMEM)


def kernel_call(kernel, name, out, ins, scratch=()):
    return pl.pallas_call(
        kernel,
        name=name,
        out_shape=out,
        in_specs=ins,
        out_specs=jax.tree.map(lambda _: VMEM, out),
        scratch_shapes=scratch,
        compiler_params=pltpu.CompilerParams(vmem_limit_bytes=16 << 20),
    )


def f32(*shape):
    return jax.ShapeDtypeStruct(shape, jnp.float32)


def line(t, vecs, part):
    return pl.ds(t * vecs * 3 + part, vecs, stride=3)


def keep(split, slot, values):
    vecs = values.shape[0]
    high = values.astype(jnp.bfloat16)
    split[slot, 0:vecs, :] = high
    split[slot, vecs : 2 * vecs, :] = (values - high.astype(jnp.float32)).astype(jnp.bfloat16)


def multiply(index_ref, tiles_ref, split, total, direct, mirror):
    seg_tiles = total.shape[0] // 3
    vecs = total.shape[1]
    slots = tiles_ref.shape[0]
    count = index_ref[2 * slots]
    size = GROUP if slots % GROUP == 0 else slots
    total[...] = jnp.zeros_like(total)

    def group(g, carry):
        parts = []
        for j in range(size):
            slot = g * size + j
            row = index_ref[slot]
            col = index_ref[slots + slot] + seg_tiles
            tile = tiles_ref[slot]
            live = slot < count
            for wanted, taken, place, dims in ((direct, col, row, NT), (mirror, row, col, NN)):
                if wanted:
                    part = lax.dot_general(split[taken], tile, dims, preferred_element_type=jnp.float32)
                    parts.append((place, jnp.where(live, part[:vecs] + part[vecs:], 0.0)))
        for place, part in parts:
            total[place] += part
        return carry

    lax.fori_loop(0, (count + (size - 1)) // size, group, 0)


def first_mirror(index_ref, tiles_ref, seg_ref, out_ref, split, total):
    seg_tiles = total.shape[0] // 3
    for t in range(seg_tiles):
        keep(split, t, seg_ref[:, t * LANE : (t + 1) * LANE])
    multiply(index_ref, tiles_ref, split, total, False, True)
    out_ref[...] = total[seg_tiles : 3 * seg_tiles]


def first_direct(index_ref, tiles_ref, block_ref, mirrored_ref, out_ref, split, total):
    seg_tiles, vecs = total.shape[0] // 3, total.shape[1]
    for t in range(2 * seg_tiles):
        keep(split, seg_tiles + t, block_ref[t // 2, :, (t % 2) * LANE : (t % 2 + 1) * LANE])
    multiply(index_ref, tiles_ref, split, total, True, False)
    for t in range(seg_tiles):
        out_ref[line(t, vecs, 0), :] = total[t]
        for half in range(2):
            out_ref[line(t, vecs, 1 + half), :] = mirrored_ref[half * seg_tiles + t]


def multiply_next(index_ref, tiles_ref, all_ref, out_ref, split, total):
    seg_tiles, vecs = total.shape[0] // 3, total.shape[1]
    for t in range(seg_tiles):
        for part in range(3):
            keep(split, part * seg_tiles + t, all_ref[line(t, vecs, part), :])
    multiply(index_ref, tiles_ref, split, total, True, True)
    for t in range(seg_tiles):
        for part in range(3):
            out_ref[line(t, vecs, part), :] = total[part * seg_tiles + t]


def line_pair(r, half, which, part):
    return pl.ds(r * half * 6 + which * 3 + part, half, stride=6)


def add_up(rows, half, index_ref, got_ref, sums_ref):
    odd = index_ref[index_ref.shape[0] - 1] == 1
    for which in range(2):
        base = which * rows
        for r in range(rows):
            sums_ref[base + r : base + r + 1, :] = jnp.sum(
                got_ref[line_pair(r, half, which, 0), :], axis=0, keepdims=True
            )
        for part in range(2):
            mirror = got_ref[line_pair(0, half, which, 1 + part), :]
            for r in range(1, rows):
                mirror = mirror + got_ref[line_pair(r, half, which, 1 + part), :]
            for core in range(2):
                place = pl.ds(base + 2 * core + part, half, stride=4)
                sums_ref[place, :] = sums_ref[place, :] + jnp.where(odd == (core == 1), mirror, 0.0)


def deal(rows, half, index_ref, mine_ref, other_ref, out_ref, own_ref):
    odd = index_ref[index_ref.shape[0] - 1] == 1
    own_ref[...] = mine_ref[...] + other_ref[...]
    for which in range(2):
        base = which * rows
        blocks = []
        for part in range(2):
            even_rows = own_ref[pl.ds(base + part, half, stride=4), :]
            odd_rows = own_ref[pl.ds(base + 2 + part, half, stride=4), :]
            blocks.append(jnp.where(odd, odd_rows, even_rows))
        for r in range(rows):
            out_ref[line_pair(r, half, which, 0), :] = jnp.broadcast_to(
                own_ref[base + r : base + r + 1, :], (half, LANE)
            )
            for part in range(2):
                out_ref[line_pair(r, half, which, 1 + part), :] = blocks[part]


def show(mine_ref, other_ref, two_ref, out_ref):
    three = mine_ref[...] + other_ref[...]
    size = three.shape[0]
    for c in range(out_ref.shape[0]):
        out_ref[c, 0:size, :] = two_ref[...]
        out_ref[c, size : 2 * size, :] = three


def dots(a, b):
    return lax.dot_general(a, b, NT, precision=HIGH, preferred_element_type=jnp.float32)


def gram_known(start_ref, one_ref, two_ref, gram_ref, basis):
    vecs = start_ref.shape[0]
    for t in range(start_ref.shape[1] // LANE):
        lanes = slice(t * LANE, (t + 1) * LANE)
        basis[0:vecs, lanes] = one_ref[line(t, vecs, 0), :]
        basis[vecs : 2 * vecs, lanes] = two_ref[line(t, vecs, 0), :]
    held = [start_ref[...], basis[0:vecs, :], basis[vecs : 2 * vecs, :]]
    parts = [dots(held[j // 2], held[(j + 1) // 2]) for j in range(2 * ITERS - 1)]
    parts.append(jnp.zeros((vecs, LANE - (2 * ITERS - 1) * vecs), jnp.float32))
    gram_ref[...] = jnp.concatenate(parts, axis=1)


def gram_last(rows, known_ref, shown_ref, out_ref, basis):
    vecs = known_ref.shape[0]
    for s in range(rows):
        lanes = slice(s * LANE, (s + 1) * LANE)
        for j in range(2):
            for which in range(2):
                taken = shown_ref[pl.ds((j * 2 + which) * rows + s, vecs // 2, stride=4 * rows), :]
                out_ref[s, 1 - j, pl.ds(which, vecs // 2, stride=2), :] = taken
            basis[j * vecs : (j + 1) * vecs, lanes] = out_ref[s, 1 - j]
    two, three = basis[0:vecs, :], basis[vecs : 2 * vecs, :]
    width = (2 * ITERS - 1) * vecs
    parts = [known_ref[...][:, :width], dots(two, three), dots(three, three)]
    parts.append(jnp.zeros((vecs, LANE - (2 * ITERS + 1) * vecs), jnp.float32))
    grams = jnp.concatenate(parts, axis=1)
    for s in range(rows):
        out_ref[s, 1] = grams


def finish(states, last_ref, turn_ref, start_ref, one_ref, two_ref, eigen_ref, ritz_ref):
    vecs = eigen_ref.shape[0]

    def mul(a, b, dims=NN):
        full = jnp.concatenate([b, jnp.zeros((LANE - b.shape[0], b.shape[1]), jnp.float32)], axis=0)
        return lax.dot_general(a, full, dims, precision=HIGH, preferred_element_type=jnp.float32)

    moments = last_ref[0, 1]
    for r in range(1, last_ref.shape[0]):
        moments = moments + last_ref[r, 1]
    moments = moments * (1.0 / states)
    hankel = jnp.concatenate(
        [moments] + [pltpu.roll(moments, LANE - j * vecs, 1) for j in range(1, ITERS)], axis=0
    )
    eye = lax.broadcasted_iota(jnp.int32, (vecs, LANE), 0) == lax.broadcasted_iota(jnp.int32, (vecs, LANE), 1)
    iterate = eye.astype(jnp.float32)
    search = None
    for i in range(ITERS):
        keep_turn, step, past = (turn_ref[i, j] for j in range(3))
        weighted = mul(iterate, hankel) if i else moments
        own = mul(weighted, iterate, NT)
        theta = mul(pltpu.roll(weighted, LANE - vecs, 1), iterate, NT)
        images = mul(pltpu.roll(weighted, LANE - 2 * vecs, 1), iterate, NT)
        terms = jnp.where(eye, images, 0.0) - 2.0 * theta * theta + theta * mul(own, theta)
        spread = jnp.maximum(jnp.sum(terms, axis=0, keepdims=True), 0.0)
        scaled = step / jnp.sqrt(spread + 1e-06)
        residual = pltpu.roll(iterate, vecs, 1) - mul(theta, iterate)
        moved = mul(scaled, residual)
        if search is not None:
            moved = moved - mul(-past, search)
        iterate = moved - mul(-keep_turn, iterate)
        search = moved
    ritz_ref[...] = theta[:, :vecs]
    for t in range(eigen_ref.shape[1] // LANE):
        lanes = slice(t * LANE, (t + 1) * LANE)
        basis = [start_ref[:, lanes], one_ref[line(t, vecs, 0), :], two_ref[line(t, vecs, 0), :], last_ref[t, 0]]
        eigen_ref[:, lanes] = mul(iterate, jnp.concatenate(basis, axis=0))


def body(tiles, tile_row, tile_col, tile_counts, start, rotation):
    tiles = tiles.reshape(tiles.shape[2:])
    slots = tiles.shape[0]
    vecs, seg_rows = start.shape
    rows = lax.axis_size("row")
    cols = lax.axis_size("col")
    seg_tiles = seg_rows // LANE
    pair = 2 * LANE
    half = cols // 2
    own_col = lax.axis_index("col")
    index = [tile_row.reshape(slots), tile_col.reshape(slots), tile_counts.reshape(1), (own_col % 2).reshape(1)]
    index = jnp.concatenate(index)
    dealt = f32(rows * cols * 3, LANE)
    work = [
        pltpu.VMEM((3 * seg_tiles, 2 * vecs, LANE), jnp.bfloat16),
        pltpu.VMEM((3 * seg_tiles, vecs, LANE), jnp.float32),
    ]
    summed = f32(2 * rows, LANE)
    same_core = [[core + 2 * c for c in range(half)] for core in range(2)]
    all_same_core = [[r * cols + c for r in range(rows) for c in group] for group in same_core]
    basis = [pltpu.VMEM((2 * vecs, seg_rows), jnp.float32)]
    corner = []
    for r in range(rows):
        for c in range(cols):
            corner.append((r * cols + c, ((r % 2) * cols + c) * cols + r // 2))

    def swap(x):
        x = x.reshape(rows * half, 6 * LANE)
        x = lax.all_to_all(x, BOTH, 0, 0, axis_index_groups=all_same_core)
        return x.reshape(rows * cols * 3, LANE)

    def reduced(x):
        add = functools.partial(add_up, rows, half)
        mine = kernel_call(add, "add_up", summed, [SMEM, VMEM])(index, swap(x))
        return mine, lax.ppermute(mine, "col", [(c, c ^ 1) for c in range(cols)])

    own_start = lax.dynamic_slice_in_dim(start, own_col * pair, pair, 1)
    index, piece = lax.optimization_barrier((index, lax.ppermute(own_start, BOTH, corner)))
    block = lax.all_to_all(jnp.broadcast_to(piece, (rows, vecs, pair)), "row", 0, 0)
    mirrored = kernel_call(
        first_mirror, "first_mirror", f32(2 * seg_tiles, vecs, LANE), [SMEM] + [VMEM] * 2, work
    )(index, tiles, start)
    sent = kernel_call(first_direct, "first_direct", dealt, [SMEM] + [VMEM] * 3, work)(
        index, tiles, block, mirrored
    )
    images = []
    for _ in range(ITERS - 1):
        given, own = kernel_call(
            functools.partial(deal, rows, half), "deal", (dealt, summed), [SMEM] + [VMEM] * 2
        )(index, *reduced(sent))
        images.append(swap(given))
        sent = kernel_call(multiply_next, "multiply_next", dealt, [SMEM] + [VMEM] * 2, work)(
            index, tiles, images[-1]
        )
    shown = kernel_call(show, "show", f32(half, 4 * rows, LANE), [VMEM] * 3)(*reduced(sent), own)
    shown = lax.all_to_all(shown, "col", 0, 0, axis_index_groups=same_core).reshape(half * 4 * rows, LANE)
    known = kernel_call(gram_known, "gram_known", f32(vecs, LANE), [VMEM] * 3, basis)(start, *images)
    last = kernel_call(
        functools.partial(gram_last, rows), "gram_last", f32(rows, 2, vecs, LANE), [VMEM] * 2, basis
    )(known, shown)
    last = lax.all_to_all(last, "row", 0, 0)
    turned = jnp.pad(jnp.swapaxes(rotation, 2, 3), ((0, 0),) * 3 + ((0, LANE - vecs),))
    return kernel_call(
        functools.partial(finish, seg_rows * rows), "finish", (f32(vecs, seg_rows), f32(vecs, vecs)), [VMEM] * 5
    )(last, turned, start, *images)


def solution(mesh):
    return jax.shard_map(
        body,
        mesh=mesh,
        in_specs=(
            P("row", "col", None, None, None),
            P("row", "col", None),
            P("row", "col", None),
            P("row", "col"),
            P(None, "row"),
            P(),
        ),
        out_specs=(P(None, "row"), P()),
        check_vma=False,
    )
```

```python
import functools

import jax
import jax.numpy as jnp
from jax import lax
from jax.experimental import pallas as pl
from jax.experimental.pallas import tpu as pltpu
from jax.sharding import PartitionSpec as P

ITERS = 3
LANE = 128
GROUP = 96
BOTH = ("row", "col")
HIGH = lax.Precision.HIGHEST
NT = (((1,), (1,)), ((), ()))
NN = (((1,), (0,)), ((), ()))
SMEM = pl.BlockSpec(memory_space=pltpu.SMEM)
VMEM = pl.BlockSpec(memory_space=pltpu.VMEM)


def kernel_call(kernel, name, out, ins, scratch=()):
    return pl.pallas_call(
        kernel,
        name=name,
        out_shape=out,
        in_specs=ins,
        out_specs=jax.tree.map(lambda _: VMEM, out),
        scratch_shapes=scratch,
        compiler_params=pltpu.CompilerParams(vmem_limit_bytes=16 << 20),
    )


def f32(*shape):
    return jax.ShapeDtypeStruct(shape, jnp.float32)


def line(t, vecs, part):
    return pl.ds(t * vecs * 3 + part, vecs, stride=3)


def keep(split, slot, values):
    vecs = values.shape[0]
    high = values.astype(jnp.bfloat16)
    split[slot, 0:vecs, :] = high
    split[slot, vecs : 2 * vecs, :] = (values - high.astype(jnp.float32)).astype(jnp.bfloat16)


def multiply(index_ref, tiles_ref, split, total, direct, mirror):
    seg_tiles = total.shape[0] // 3
    vecs = total.shape[1]
    slots = tiles_ref.shape[0]
    count = index_ref[2 * slots]
    size = GROUP if slots % GROUP == 0 else slots
    total[...] = jnp.zeros_like(total)

    def group(g, carry):
        parts = []
        for j in range(size):
            slot = g * size + j
            row = index_ref[slot]
            col = index_ref[slots + slot] + seg_tiles
            tile = tiles_ref[slot]
            live = slot < count
            for wanted, taken, place, dims in ((direct, col, row, NT), (mirror, row, col, NN)):
                if wanted:
                    part = lax.dot_general(split[taken], tile, dims, preferred_element_type=jnp.float32)
                    parts.append((place, jnp.where(live, part[:vecs] + part[vecs:], 0.0)))
        for place, part in parts:
            total[place] += part
        return carry

    lax.fori_loop(0, (count + (size - 1)) // size, group, 0)


def first_mirror(index_ref, tiles_ref, seg_ref, out_ref, split, total):
    seg_tiles = total.shape[0] // 3
    for t in range(seg_tiles):
        keep(split, t, seg_ref[:, t * LANE : (t + 1) * LANE])
    multiply(index_ref, tiles_ref, split, total, False, True)
    out_ref[...] = total[seg_tiles : 3 * seg_tiles]


def first_direct(index_ref, tiles_ref, block_ref, mirrored_ref, out_ref, split, total):
    seg_tiles, vecs = total.shape[0] // 3, total.shape[1]
    for t in range(2 * seg_tiles):
        keep(split, seg_tiles + t, block_ref[t // 2, :, (t % 2) * LANE : (t % 2 + 1) * LANE])
    multiply(index_ref, tiles_ref, split, total, True, False)
    for t in range(seg_tiles):
        out_ref[line(t, vecs, 0), :] = total[t]
        for half in range(2):
            out_ref[line(t, vecs, 1 + half), :] = mirrored_ref[half * seg_tiles + t]


def multiply_next(index_ref, tiles_ref, all_ref, out_ref, split, total):
    seg_tiles, vecs = total.shape[0] // 3, total.shape[1]
    for t in range(seg_tiles):
        for part in range(3):
            keep(split, part * seg_tiles + t, all_ref[line(t, vecs, part), :])
    multiply(index_ref, tiles_ref, split, total, True, True)
    for t in range(seg_tiles):
        for part in range(3):
            out_ref[line(t, vecs, part), :] = total[part * seg_tiles + t]


def add_up(rows, cols, got_ref, sums):
    for r in range(rows):
        half = r % 2
        sums[r // 2 : r // 2 + 1, half * LANE : (half + 1) * LANE] = jnp.sum(
            got_ref[line(r, cols, 0), :], axis=0, keepdims=True
        )
    for half in range(2):
        mirror = got_ref[line(0, cols, 1 + half), :]
        for r in range(1, rows):
            mirror = mirror + got_ref[line(r, cols, 1 + half), :]
        lanes = slice(half * LANE, (half + 1) * LANE)
        sums[:, lanes] = sums[:, lanes] + mirror


def sum_and_deal(rows, cols, got_ref, out_ref, own_ref, sums):
    add_up(rows, cols, got_ref, sums)
    for half in range(2):
        own_ref[pl.ds(half, cols, stride=2), :] = sums[:, half * LANE : (half + 1) * LANE]
    for r in range(rows):
        half = r % 2
        out_ref[line(r, cols, 0), :] = jnp.broadcast_to(
            sums[r // 2 : r // 2 + 1, half * LANE : (half + 1) * LANE], (cols, LANE)
        )
        for half in range(2):
            out_ref[line(r, cols, 1 + half), :] = sums[:, half * LANE : (half + 1) * LANE]


def sum_and_show(rows, cols, got_ref, two_ref, out_ref, sums):
    add_up(rows, cols, got_ref, sums)
    for c in range(cols):
        out_ref[c, 0:rows, :] = two_ref[...]
        for half in range(2):
            out_ref[c, pl.ds(rows + half, cols, stride=2), :] = sums[:, half * LANE : (half + 1) * LANE]


def dots(a, b):
    return lax.dot_general(a, b, NT, precision=HIGH, preferred_element_type=jnp.float32)


def gram_known(start_ref, one_ref, two_ref, gram_ref, basis):
    vecs = start_ref.shape[0]
    for t in range(start_ref.shape[1] // LANE):
        lanes = slice(t * LANE, (t + 1) * LANE)
        basis[0:vecs, lanes] = one_ref[line(t, vecs, 0), :]
        basis[vecs : 2 * vecs, lanes] = two_ref[line(t, vecs, 0), :]
    held = [start_ref[...], basis[0:vecs, :], basis[vecs : 2 * vecs, :]]
    parts = [dots(held[j // 2], held[(j + 1) // 2]) for j in range(2 * ITERS - 1)]
    parts.append(jnp.zeros((vecs, LANE - (2 * ITERS - 1) * vecs), jnp.float32))
    gram_ref[...] = jnp.concatenate(parts, axis=1)


def gram_last(rows, known_ref, shown_ref, out_ref, basis):
    vecs = known_ref.shape[0]
    for s in range(rows):
        lanes = slice(s * LANE, (s + 1) * LANE)
        basis[0:vecs, lanes] = shown_ref[pl.ds(s, vecs, stride=2 * rows), :]
        three = shown_ref[pl.ds(rows + s, vecs, stride=2 * rows), :]
        basis[vecs : 2 * vecs, lanes] = three
        out_ref[s, 0] = three
    width = (2 * ITERS - 1) * vecs
    both = dots(basis[...], basis[vecs : 2 * vecs, :])
    parts = [known_ref[...][:, :width], both[:vecs], both[vecs:]]
    parts.append(jnp.zeros((vecs, LANE - (2 * ITERS + 1) * vecs), jnp.float32))
    grams = jnp.concatenate(parts, axis=1)
    for s in range(rows):
        out_ref[s, 1] = grams


def finish(states, last_ref, turn_ref, start_ref, one_ref, two_ref, eigen_ref, ritz_ref):
    vecs = eigen_ref.shape[0]

    def mul(a, b, dims=NN):
        full = jnp.concatenate([b, jnp.zeros((LANE - b.shape[0], b.shape[1]), jnp.float32)], axis=0)
        return lax.dot_general(a, full, dims, precision=HIGH, preferred_element_type=jnp.float32)

    moments = last_ref[0, 1]
    for r in range(1, last_ref.shape[0]):
        moments = moments + last_ref[r, 1]
    moments = moments * (1.0 / states)
    hankel = jnp.concatenate(
        [moments] + [pltpu.roll(moments, LANE - j * vecs, 1) for j in range(1, ITERS)], axis=0
    )
    eye = lax.broadcasted_iota(jnp.int32, (vecs, LANE), 0) == lax.broadcasted_iota(jnp.int32, (vecs, LANE), 1)
    iterate = eye.astype(jnp.float32)
    search = None
    for i in range(ITERS):
        keep_turn, step, past = (turn_ref[i, j] for j in range(3))
        weighted = mul(iterate, hankel) if i else moments
        own = mul(weighted, iterate, NT)
        theta = mul(pltpu.roll(weighted, LANE - vecs, 1), iterate, NT)
        images = mul(pltpu.roll(weighted, LANE - 2 * vecs, 1), iterate, NT)
        terms = jnp.where(eye, images, 0.0) - 2.0 * theta * theta + theta * mul(own, theta)
        spread = jnp.maximum(jnp.sum(terms, axis=0, keepdims=True), 0.0)
        scaled = step / jnp.sqrt(spread + 1e-06)
        residual = pltpu.roll(iterate, vecs, 1) - mul(theta, iterate)
        moved = mul(scaled, residual)
        if search is not None:
            moved = moved - mul(-past, search)
        iterate = moved - mul(-keep_turn, iterate)
        search = moved
    ritz_ref[...] = theta[:, :vecs]
    used = (ITERS + 1) * vecs
    terms = []
    rest = iterate[:, :used]
    for _ in range(3):
        terms.append(rest.astype(jnp.bfloat16))
        rest = rest - terms[-1].astype(jnp.float32)
    factors = jnp.concatenate(terms, axis=0)
    for t in range(eigen_ref.shape[1] // LANE):
        lanes = slice(t * LANE, (t + 1) * LANE)
        basis = [start_ref[:, lanes], one_ref[line(t, vecs, 0), :], two_ref[line(t, vecs, 0), :], last_ref[t, 0]]
        basis = jnp.concatenate(basis, axis=0)
        high = basis.astype(jnp.bfloat16)
        low = (basis - high.astype(jnp.float32)).astype(jnp.bfloat16)
        large = lax.dot_general(factors, high, NN, preferred_element_type=jnp.float32)
        small = lax.dot_general(factors[: 2 * vecs], low, NN, preferred_element_type=jnp.float32)
        small = small[:vecs] + small[vecs:] + large[2 * vecs :]
        eigen_ref[:, lanes] = large[:vecs] + (large[vecs : 2 * vecs] + small)


def body(tiles, tile_row, tile_col, tile_counts, start, rotation):
    tiles = tiles.reshape(tiles.shape[2:])
    slots = tiles.shape[0]
    vecs, seg_rows = start.shape
    rows = lax.axis_size("row")
    cols = lax.axis_size("col")
    seg_tiles = seg_rows // LANE
    pair = 2 * LANE
    index = jnp.concatenate([tile_row.reshape(slots), tile_col.reshape(slots), tile_counts.reshape(1)])
    own_col = lax.axis_index("col")
    dealt = f32(rows * cols * 3, LANE)
    work = [
        pltpu.VMEM((3 * seg_tiles, 2 * vecs, LANE), jnp.bfloat16),
        pltpu.VMEM((3 * seg_tiles, vecs, LANE), jnp.float32),
    ]
    sums = [pltpu.VMEM((cols, pair), jnp.float32)]
    basis = [pltpu.VMEM((2 * vecs, seg_rows), jnp.float32)]
    corner = []
    for r in range(rows):
        for c in range(cols):
            corner.append((r * cols + c, ((r % 2) * cols + c) * cols + r // 2))

    def swap(x):
        moved = lax.all_to_all(x.reshape(rows * cols, 3 * LANE), BOTH, 0, 0)
        return moved.reshape(rows * cols * 3, LANE)

    own_start = lax.dynamic_slice_in_dim(start, own_col * pair, pair, 1)
    index, piece = lax.optimization_barrier((index, lax.ppermute(own_start, BOTH, corner)))
    block = lax.all_to_all(jnp.broadcast_to(piece, (rows, vecs, pair)), "row", 0, 0)
    mirrored = kernel_call(
        first_mirror, "first_mirror", f32(2 * seg_tiles, vecs, LANE), [SMEM] + [VMEM] * 2, work
    )(index, tiles, start)
    sent = kernel_call(first_direct, "first_direct", dealt, [SMEM] + [VMEM] * 3, work)(
        index, tiles, block, mirrored
    )
    images = []
    for _ in range(ITERS - 1):
        given, own = kernel_call(
            functools.partial(sum_and_deal, rows, cols), "sum_and_deal", (dealt, f32(rows, LANE)), [VMEM], sums
        )(swap(sent))
        images.append(swap(given))
        sent = kernel_call(multiply_next, "multiply_next", dealt, [SMEM] + [VMEM] * 2, work)(
            index, tiles, images[-1]
        )
    shown = kernel_call(
        functools.partial(sum_and_show, rows, cols), "sum_and_show", f32(cols, 2 * rows, LANE), [VMEM] * 2, sums
    )(swap(sent), own)
    shown = lax.all_to_all(shown, "col", 0, 0).reshape(cols * 2 * rows, LANE)
    known = kernel_call(gram_known, "gram_known", f32(vecs, LANE), [VMEM] * 3, basis)(start, *images)
    last = kernel_call(
        functools.partial(gram_last, rows), "gram_last", f32(rows, 2, vecs, LANE), [VMEM] * 2, basis
    )(known, shown)
    last = lax.all_to_all(last, "row", 0, 0)
    turned = jnp.pad(jnp.swapaxes(rotation, 2, 3), ((0, 0),) * 3 + ((0, LANE - vecs),))
    return kernel_call(
        functools.partial(finish, seg_rows * rows), "finish", (f32(vecs, seg_rows), f32(vecs, vecs)), [VMEM] * 5
    )(last, turned, start, *images)


def solution(mesh):
    return jax.shard_map(
        body,
        mesh=mesh,
        in_specs=(
            P("row", "col", None, None, None),
            P("row", "col", None),
            P("row", "col", None),
            P("row", "col"),
            P(None, "row"),
            P(),
        ),
        out_specs=(P(None, "row"), P()),
        check_vma=False,
    )
```

```python
import functools

import jax
import jax.numpy as jnp
from jax import lax
from jax.experimental import pallas as pl
from jax.experimental.pallas import tpu as pltpu
from jax.sharding import PartitionSpec as P

ITERS = 3
LANE = 128
GROUP = 32
BOTH = ("row", "col")
HIGH = lax.Precision.HIGHEST
NT = (((1,), (1,)), ((), ()))
NN = (((1,), (0,)), ((), ()))
SMEM = pl.BlockSpec(memory_space=pltpu.SMEM)
VMEM = pl.BlockSpec(memory_space=pltpu.VMEM)


def kernel_call(kernel, name, out, ins, scratch=()):
    return pl.pallas_call(
        kernel,
        name=name,
        out_shape=out,
        in_specs=ins,
        out_specs=jax.tree.map(lambda _: VMEM, out),
        scratch_shapes=scratch,
        compiler_params=pltpu.CompilerParams(vmem_limit_bytes=16 << 20),
    )


def f32(*shape):
    return jax.ShapeDtypeStruct(shape, jnp.float32)


def line(t, vecs, part):
    return pl.ds(t * vecs * 3 + part, vecs, stride=3)


def keep(split, slot, values):
    vecs = values.shape[0]
    high = values.astype(jnp.bfloat16)
    split[slot, 0:vecs, :] = high
    split[slot, vecs : 2 * vecs, :] = (values - high.astype(jnp.float32)).astype(jnp.bfloat16)


def multiply(index_ref, tiles_ref, split, total, direct, mirror):
    seg_tiles = total.shape[0] // 3
    vecs = total.shape[1]
    slots = tiles_ref.shape[0]
    count = index_ref[2 * slots]
    size = GROUP if slots % GROUP == 0 else slots
    total[...] = jnp.zeros_like(total)

    def group(g, carry):
        parts = []
        for j in range(size):
            slot = g * size + j
            row = index_ref[slot]
            col = index_ref[slots + slot] + seg_tiles
            tile = tiles_ref[slot]
            live = slot < count
            for wanted, taken, place, dims in ((direct, col, row, NT), (mirror, row, col, NN)):
                if wanted:
                    part = lax.dot_general(split[taken], tile, dims, preferred_element_type=jnp.float32)
                    parts.append((place, jnp.where(live, part[:vecs] + part[vecs:], 0.0)))
        for place, part in parts:
            total[place] += part
        return carry

    lax.fori_loop(0, (count + (size - 1)) // size, group, 0)


def first_mirror(index_ref, tiles_ref, seg_ref, out_ref, split, total):
    seg_tiles = total.shape[0] // 3
    for t in range(seg_tiles):
        keep(split, t, seg_ref[:, t * LANE : (t + 1) * LANE])
    multiply(index_ref, tiles_ref, split, total, False, True)
    out_ref[...] = total[seg_tiles : 3 * seg_tiles]


def first_direct(index_ref, tiles_ref, block_ref, mirrored_ref, out_ref, split, total):
    seg_tiles, vecs = total.shape[0] // 3, total.shape[1]
    for t in range(2 * seg_tiles):
        keep(split, seg_tiles + t, block_ref[t // 2, :, (t % 2) * LANE : (t % 2 + 1) * LANE])
    multiply(index_ref, tiles_ref, split, total, True, False)
    for t in range(seg_tiles):
        out_ref[line(t, vecs, 0), :] = total[t]
        for half in range(2):
            out_ref[line(t, vecs, 1 + half), :] = mirrored_ref[half * seg_tiles + t]


def multiply_all(index_ref, tiles_ref, all_ref, split, total):
    seg_tiles, vecs = total.shape[0] // 3, total.shape[1]
    for t in range(seg_tiles):
        for part in range(3):
            keep(split, part * seg_tiles + t, all_ref[line(t, vecs, part), :])
    multiply(index_ref, tiles_ref, split, total, True, True)


def multiply_next(index_ref, tiles_ref, all_ref, out_ref, split, total):
    seg_tiles, vecs = total.shape[0] // 3, total.shape[1]
    multiply_all(index_ref, tiles_ref, all_ref, split, total)
    for t in range(seg_tiles):
        for part in range(3):
            out_ref[line(t, vecs, part), :] = total[part * seg_tiles + t]


def multiply_last(index_ref, tiles_ref, all_ref, direct_ref, mirror_ref, split, total):
    multiply_all(index_ref, tiles_ref, all_ref, split, total)
    for refs, base in ((direct_ref, 0), (mirror_ref, total.shape[0] // 3)):
        for t in range(2 * refs.shape[0]):
            refs[t // 2, :, (t % 2) * LANE : (t % 2 + 1) * LANE] = total[base + t]


def add_up(rows, cols, got_ref, sums):
    for r in range(rows):
        half = r % 2
        sums[r // 2 : r // 2 + 1, half * LANE : (half + 1) * LANE] = jnp.sum(
            got_ref[line(r, cols, 0), :], axis=0, keepdims=True
        )
    for half in range(2):
        mirror = got_ref[line(0, cols, 1 + half), :]
        for r in range(1, rows):
            mirror = mirror + got_ref[line(r, cols, 1 + half), :]
        lanes = slice(half * LANE, (half + 1) * LANE)
        sums[:, lanes] = sums[:, lanes] + mirror


def sum_and_deal(rows, cols, got_ref, out_ref, sums):
    add_up(rows, cols, got_ref, sums)
    for r in range(rows):
        half = r % 2
        out_ref[line(r, cols, 0), :] = jnp.broadcast_to(
            sums[r // 2 : r // 2 + 1, half * LANE : (half + 1) * LANE], (cols, LANE)
        )
        for half in range(2):
            out_ref[line(r, cols, 1 + half), :] = sums[:, half * LANE : (half + 1) * LANE]


def gram(zero_ref, one_ref, two_ref, three_ref, gram_ref):
    vecs = three_ref.shape[0]
    basis = [zero_ref[...], one_ref[...], two_ref[...], three_ref[...]]
    parts = []
    for j in range(ITERS + 1):
        others = jnp.concatenate(basis[j : j + 2], axis=0)
        parts.append(
            lax.dot_general(basis[j], others, NT, precision=HIGH, preferred_element_type=jnp.float32)
        )
    parts.append(jnp.zeros((vecs, LANE - (2 * ITERS + 1) * vecs), jnp.float32))
    gram_ref[...] = jnp.concatenate(parts, axis=1)


def finish(states, last_ref, turn_ref, start_ref, one_ref, two_ref, eigen_ref, ritz_ref):
    vecs = eigen_ref.shape[0]

    def mul(a, b, dims=NN):
        full = jnp.concatenate([b, jnp.zeros((LANE - b.shape[0], b.shape[1]), jnp.float32)], axis=0)
        return lax.dot_general(a, full, dims, precision=HIGH, preferred_element_type=jnp.float32)

    moments = last_ref[0, 2]
    for c in range(1, last_ref.shape[0]):
        moments = moments + last_ref[c, 2]
    moments = moments * (1.0 / states)
    hankel = jnp.concatenate(
        [moments] + [pltpu.roll(moments, LANE - j * vecs, 1) for j in range(1, ITERS)], axis=0
    )
    eye = lax.broadcasted_iota(jnp.int32, (vecs, LANE), 0) == lax.broadcasted_iota(jnp.int32, (vecs, LANE), 1)
    iterate = eye.astype(jnp.float32)
    search = None
    for i in range(ITERS):
        keep_turn, step, past = (turn_ref[i, j] for j in range(3))
        weighted = mul(iterate, hankel) if i else moments
        own = mul(weighted, iterate, NT)
        theta = mul(pltpu.roll(weighted, LANE - vecs, 1), iterate, NT)
        images = mul(pltpu.roll(weighted, LANE - 2 * vecs, 1), iterate, NT)
        terms = jnp.where(eye, images, 0.0) - 2.0 * theta * theta + theta * mul(own, theta)
        spread = jnp.maximum(jnp.sum(terms, axis=0, keepdims=True), 0.0)
        scaled = step / jnp.sqrt(spread + 1e-06)
        residual = pltpu.roll(iterate, vecs, 1) - mul(theta, iterate)
        moved = mul(scaled, residual)
        if search is not None:
            moved = moved - mul(-past, search)
        iterate = moved - mul(-keep_turn, iterate)
        search = moved
    ritz_ref[...] = theta[:, :vecs]
    used = (ITERS + 1) * vecs
    terms = []
    rest = iterate[:, :used]
    for _ in range(3):
        terms.append(rest.astype(jnp.bfloat16))
        rest = rest - terms[-1].astype(jnp.float32)
    factors = jnp.concatenate(terms, axis=0)
    for t in range(eigen_ref.shape[1] // LANE):
        lanes = slice(t * LANE, (t + 1) * LANE)
        basis = [start_ref[:, lanes], one_ref[line(t, vecs, 0), :], two_ref[line(t, vecs, 0), :], last_ref[t // 2, t % 2]]
        basis = jnp.concatenate(basis, axis=0)
        high = basis.astype(jnp.bfloat16)
        low = (basis - high.astype(jnp.float32)).astype(jnp.bfloat16)
        large = lax.dot_general(factors, high, NN, preferred_element_type=jnp.float32)
        small = lax.dot_general(factors[: 2 * vecs], low, NN, preferred_element_type=jnp.float32)
        small = small[:vecs] + small[vecs:] + large[2 * vecs :]
        eigen_ref[:, lanes] = large[:vecs] + (large[vecs : 2 * vecs] + small)


def body(tiles, tile_row, tile_col, tile_counts, start, rotation):
    tiles = tiles.reshape(tiles.shape[2:])
    slots = tiles.shape[0]
    vecs, seg_rows = start.shape
    rows = lax.axis_size("row")
    cols = lax.axis_size("col")
    seg_tiles = seg_rows // LANE
    pair = 2 * LANE
    index = jnp.concatenate([tile_row.reshape(slots), tile_col.reshape(slots), tile_counts.reshape(1)])
    own_col = lax.axis_index("col")
    dealt = f32(rows * cols * 3, LANE)
    work = [
        pltpu.VMEM((3 * seg_tiles, 2 * vecs, LANE), jnp.bfloat16),
        pltpu.VMEM((3 * seg_tiles, vecs, LANE), jnp.float32),
    ]
    sums = [pltpu.VMEM((cols, pair), jnp.float32)]
    corner = []
    for r in range(rows):
        for c in range(cols):
            corner.append((r * cols + c, ((r % 2) * cols + c) * cols + r // 2))

    def swap(x):
        moved = lax.all_to_all(x.reshape(rows * cols, 3 * LANE), BOTH, 0, 0)
        return moved.reshape(rows * cols * 3, LANE)

    def own_block_piece(x):
        pairs = seg_tiles // 2
        own_row = lax.axis_index("row")
        size = 2 * vecs * 3
        x = lax.dynamic_slice_in_dim(x, (own_row % pairs) * size, size, 0).reshape(2, vecs, 3, LANE)
        x = jnp.where(own_row < pairs, x[:, :, 1], x[:, :, 2])
        return jnp.concatenate([x[0], x[1]], axis=1)

    def to_all(x, axis):
        count = lax.axis_size(axis)
        return lax.all_to_all(jnp.broadcast_to(x, (count,) + x.shape), axis, 0, 0)

    own_start = lax.dynamic_slice_in_dim(start, own_col * pair, pair, 1)
    index, piece = lax.optimization_barrier((index, lax.ppermute(own_start, BOTH, corner)))
    block = to_all(piece, "row")
    mirrored = kernel_call(
        first_mirror, "first_mirror", f32(2 * seg_tiles, vecs, LANE), [SMEM] + [VMEM] * 2, work
    )(index, tiles, start)
    sent = kernel_call(first_direct, "first_direct", dealt, [SMEM] + [VMEM] * 3, work)(
        index, tiles, block, mirrored
    )
    images = []
    for i in range(ITERS - 1):
        given = kernel_call(
            functools.partial(sum_and_deal, rows, cols), "sum_and_deal", dealt, [VMEM], sums
        )(swap(sent))
        images.append(swap(given))
        if i < ITERS - 2:
            sent = kernel_call(multiply_next, "multiply_next", dealt, [SMEM] + [VMEM] * 2, work)(
                index, tiles, images[-1]
            )
    direct, mirror = kernel_call(
        multiply_last, "multiply_last", (f32(cols, vecs, pair), f32(rows, vecs, pair)), [SMEM] + [VMEM] * 2, work
    )(index, tiles, images[-1])

    direct = jnp.sum(lax.all_to_all(direct, "col", 0, 0), axis=0)
    direct, mirror = lax.optimization_barrier((direct, mirror))
    direct = lax.ppermute(direct, BOTH, corner)
    last = jnp.sum(lax.all_to_all(mirror, "row", 0, 0), axis=0) + direct
    own = [own_block_piece(image) for image in images]
    grams = kernel_call(gram, "gram", f32(vecs, LANE), [VMEM] * 4)(piece, *own, last)
    last = lax.ppermute(last, BOTH, [(to, at) for at, to in corner])
    grams = jnp.sum(to_all(grams, "row"), axis=0)
    last = to_all(jnp.stack([last[:, :LANE], last[:, LANE:], grams]), "col")
    turned = jnp.pad(jnp.swapaxes(rotation, 2, 3), ((0, 0),) * 3 + ((0, LANE - vecs),))
    return kernel_call(
        functools.partial(finish, seg_rows * rows), "finish", (f32(vecs, seg_rows), f32(vecs, vecs)), [VMEM] * 5
    )(last, turned, start, *images)


def solution(mesh):
    return jax.shard_map(
        body,
        mesh=mesh,
        in_specs=(
            P("row", "col", None, None, None),
            P("row", "col", None),
            P("row", "col", None),
            P("row", "col"),
            P(None, "row"),
            P(),
        ),
        out_specs=(P(None, "row"), P()),
        check_vma=False,
    )
```

```python
import functools

import jax
import jax.numpy as jnp
from jax import lax
from jax.experimental import pallas as pl
from jax.experimental.pallas import tpu as pltpu
from jax.sharding import PartitionSpec as P

ITERS = 3
LANE = 128
GROUP = 32
BOTH = ("row", "col")
HIGH = lax.Precision.HIGHEST
NT = (((1,), (1,)), ((), ()))
NN = (((1,), (0,)), ((), ()))
SMEM = pl.BlockSpec(memory_space=pltpu.SMEM)
VMEM = pl.BlockSpec(memory_space=pltpu.VMEM)


def kernel_call(kernel, name, out, ins, scratch=()):
    return pl.pallas_call(
        kernel,
        name=name,
        out_shape=out,
        in_specs=ins,
        out_specs=jax.tree.map(lambda _: VMEM, out),
        scratch_shapes=scratch,
        compiler_params=pltpu.CompilerParams(vmem_limit_bytes=16 << 20),
    )


def f32(*shape):
    return jax.ShapeDtypeStruct(shape, jnp.float32)


def keep(split, slot, values):
    vecs = values.shape[0]
    high = values.astype(jnp.bfloat16)
    split[slot, 0:vecs, :] = high
    split[slot, vecs : 2 * vecs, :] = (values - high.astype(jnp.float32)).astype(jnp.bfloat16)


def multiply(index_ref, tiles_ref, split, total, direct, mirror):
    seg_tiles = total.shape[0] // 3
    vecs = total.shape[1]
    slots = tiles_ref.shape[0]
    count = index_ref[2 * slots]
    size = GROUP if slots % GROUP == 0 else slots
    total[...] = jnp.zeros_like(total)

    def group(g, carry):
        parts = []
        for j in range(size):
            slot = g * size + j
            row = index_ref[slot]
            col = index_ref[slots + slot] + seg_tiles
            tile = tiles_ref[slot]
            live = slot < count
            for wanted, taken, place, dims in ((direct, col, row, NT), (mirror, row, col, NN)):
                if wanted:
                    part = lax.dot_general(split[taken], tile, dims, preferred_element_type=jnp.float32)
                    parts.append((place, jnp.where(live, part[:vecs] + part[vecs:], 0.0)))
        for place, part in parts:
            total[place] += part
        return carry

    lax.fori_loop(0, (count + (size - 1)) // size, group, 0)


def halves(ref, t):
    return ref.at[t // 2, :, (t % 2) * LANE : (t % 2 + 1) * LANE]


def first_mirror(index_ref, tiles_ref, seg_ref, mirror_ref, split, total):
    seg_tiles = total.shape[0] // 3
    for t in range(seg_tiles):
        keep(split, t, seg_ref[:, t * LANE : (t + 1) * LANE])
    multiply(index_ref, tiles_ref, split, total, False, True)
    for t in range(2 * seg_tiles):
        halves(mirror_ref, t)[...] = total[seg_tiles + t]


def first_direct(index_ref, tiles_ref, block_ref, direct_ref, split, total):
    seg_tiles = total.shape[0] // 3
    for t in range(2 * seg_tiles):
        keep(split, seg_tiles + t, halves(block_ref, t)[...])
    multiply(index_ref, tiles_ref, split, total, True, False)
    for t in range(seg_tiles):
        halves(direct_ref, t)[...] = total[t]


def multiply_both(index_ref, tiles_ref, seg_ref, block_ref, direct_ref, mirror_ref, split, total):
    seg_tiles = total.shape[0] // 3
    for t in range(seg_tiles):
        keep(split, t, halves(seg_ref, t)[...])
    for t in range(2 * seg_tiles):
        keep(split, seg_tiles + t, halves(block_ref, t)[...])
    multiply(index_ref, tiles_ref, split, total, True, True)
    for t in range(seg_tiles):
        halves(direct_ref, t)[...] = total[t]
    for t in range(2 * seg_tiles):
        halves(mirror_ref, t)[...] = total[seg_tiles + t]


def gram(zero_ref, one_ref, two_ref, three_ref, gram_ref):
    vecs = three_ref.shape[0]
    basis = [zero_ref[...], one_ref[...], two_ref[...], three_ref[...]]
    parts = []
    for j in range(ITERS + 1):
        others = jnp.concatenate(basis[j : j + 2], axis=0)
        parts.append(
            lax.dot_general(basis[j], others, NT, precision=HIGH, preferred_element_type=jnp.float32)
        )
    parts.append(jnp.zeros((vecs, LANE - (2 * ITERS + 1) * vecs), jnp.float32))
    gram_ref[...] = jnp.concatenate(parts, axis=1)


def finish(states, last_ref, turn_ref, start_ref, one_ref, two_ref, eigen_ref, ritz_ref):
    vecs = eigen_ref.shape[0]

    def mul(a, b, dims=NN):
        full = jnp.concatenate([b, jnp.zeros((LANE - b.shape[0], b.shape[1]), jnp.float32)], axis=0)
        return lax.dot_general(a, full, dims, precision=HIGH, preferred_element_type=jnp.float32)

    moments = last_ref[0, 2]
    for c in range(1, last_ref.shape[0]):
        moments = moments + last_ref[c, 2]
    moments = moments * (1.0 / states)
    hankel = jnp.concatenate(
        [moments] + [pltpu.roll(moments, LANE - j * vecs, 1) for j in range(1, ITERS)], axis=0
    )
    eye = lax.broadcasted_iota(jnp.int32, (vecs, LANE), 0) == lax.broadcasted_iota(jnp.int32, (vecs, LANE), 1)
    iterate = eye.astype(jnp.float32)
    search = None
    for i in range(ITERS):
        keep_turn, step, past = (turn_ref[i, j] for j in range(3))
        weighted = mul(iterate, hankel) if i else moments
        own = mul(weighted, iterate, NT)
        theta = mul(pltpu.roll(weighted, LANE - vecs, 1), iterate, NT)
        images = mul(pltpu.roll(weighted, LANE - 2 * vecs, 1), iterate, NT)
        terms = jnp.where(eye, images, 0.0) - 2.0 * theta * theta + theta * mul(own, theta)
        spread = jnp.maximum(jnp.sum(terms, axis=0, keepdims=True), 0.0)
        scaled = step / jnp.sqrt(spread + 1e-06)
        residual = pltpu.roll(iterate, vecs, 1) - mul(theta, iterate)
        moved = mul(scaled, residual)
        if search is not None:
            moved = moved - mul(-past, search)
        iterate = moved - mul(-keep_turn, iterate)
        search = moved
    ritz_ref[...] = theta[:, :vecs]
    used = (ITERS + 1) * vecs
    terms = []
    rest = iterate[:, :used]
    for _ in range(3):
        terms.append(rest.astype(jnp.bfloat16))
        rest = rest - terms[-1].astype(jnp.float32)
    factors = jnp.concatenate(terms, axis=0)
    for t in range(eigen_ref.shape[1] // LANE):
        lanes = slice(t * LANE, (t + 1) * LANE)
        basis = [start_ref[:, lanes], halves(one_ref, t)[...], halves(two_ref, t)[...], last_ref[t // 2, t % 2]]
        basis = jnp.concatenate(basis, axis=0)
        high = basis.astype(jnp.bfloat16)
        low = (basis - high.astype(jnp.float32)).astype(jnp.bfloat16)
        large = lax.dot_general(factors, high, NN, preferred_element_type=jnp.float32)
        small = lax.dot_general(factors[: 2 * vecs], low, NN, preferred_element_type=jnp.float32)
        small = small[:vecs] + small[vecs:] + large[2 * vecs :]
        eigen_ref[:, lanes] = large[:vecs] + (large[vecs : 2 * vecs] + small)


def body(tiles, tile_row, tile_col, tile_counts, start, rotation):
    tiles = tiles.reshape(tiles.shape[2:])
    slots = tiles.shape[0]
    vecs, seg_rows = start.shape
    rows = lax.axis_size("row")
    cols = lax.axis_size("col")
    seg_tiles = seg_rows // LANE
    pair = 2 * LANE
    index = jnp.concatenate([tile_row.reshape(slots), tile_col.reshape(slots), tile_counts.reshape(1)])
    own_col = lax.axis_index("col")
    direct_shape, mirror_shape = f32(cols, vecs, pair), f32(rows, vecs, pair)
    work = [
        pltpu.VMEM((3 * seg_tiles, 2 * vecs, LANE), jnp.bfloat16),
        pltpu.VMEM((3 * seg_tiles, vecs, LANE), jnp.float32),
    ]
    corner = []
    for r in range(rows):
        for c in range(cols):
            corner.append((r * cols + c, ((r % 2) * cols + c) * cols + r // 2))
    back = [(to, at) for at, to in corner]

    def to_block(piece):
        return lax.ppermute(piece, BOTH, corner)

    def to_seg(piece):
        return lax.ppermute(piece, BOTH, back)

    def summed(x, axis):
        return jnp.sum(lax.all_to_all(x, axis, 0, 0), axis=0)

    def to_all(x, axis):
        count = lax.axis_size(axis)
        return lax.all_to_all(jnp.broadcast_to(x, (count,) + x.shape), axis, 0, 0)

    def both(seg, block):
        return kernel_call(
            multiply_both, "multiply_both", (direct_shape, mirror_shape), [SMEM] + [VMEM] * 3, work
        )(index, tiles, seg, block)

    zero = to_block(lax.dynamic_slice_in_dim(start, own_col * pair, pair, 1))
    mirror = kernel_call(first_mirror, "first_mirror", mirror_shape, [SMEM] + [VMEM] * 2, work)(index, tiles, start)
    mirror, zero = lax.optimization_barrier((summed(mirror, "row"), zero))
    block, mirror_back = lax.optimization_barrier((to_all(zero, "row"), to_seg(mirror)))
    direct = kernel_call(first_direct, "first_direct", direct_shape, [SMEM] + [VMEM] * 2, work)(index, tiles, block)
    direct = summed(direct, "col")
    one_seg = to_all(direct + mirror_back, "col")
    one_seg, one = lax.optimization_barrier((one_seg, mirror + to_block(direct)))
    direct, mirror = both(one_seg, to_all(one, "row"))

    direct, mirror = lax.optimization_barrier((summed(direct, "col"), mirror))
    two = to_block(direct) + summed(mirror, "row")
    block, two_seg = lax.optimization_barrier((to_all(two, "row"), to_seg(two)))
    two_seg = to_all(two_seg, "col")
    direct, mirror = both(two_seg, block)

    direct, mirror = lax.optimization_barrier((summed(direct, "col"), mirror))
    three = to_block(direct) + summed(mirror, "row")
    grams = kernel_call(gram, "gram", f32(vecs, LANE), [VMEM] * 4)(zero, one, two, three)
    grams = jnp.sum(to_all(grams, "row"), axis=0)
    three = to_seg(three)
    last = to_all(jnp.stack([three[:, :LANE], three[:, LANE:], grams]), "col")
    turned = jnp.pad(jnp.swapaxes(rotation, 2, 3), ((0, 0),) * 3 + ((0, LANE - vecs),))
    return kernel_call(
        functools.partial(finish, seg_rows * rows), "finish", (f32(vecs, seg_rows), f32(vecs, vecs)), [VMEM] * 5
    )(last, turned, start, one_seg, two_seg)


def solution(mesh):
    return jax.shard_map(
        body,
        mesh=mesh,
        in_specs=(
            P("row", "col", None, None, None),
            P("row", "col", None),
            P("row", "col", None),
            P("row", "col"),
            P(None, "row"),
            P(),
        ),
        out_specs=(P(None, "row"), P()),
        check_vma=False,
    )
```

```python
import functools

import jax
import jax.numpy as jnp
from jax import lax
from jax.experimental import pallas as pl
from jax.experimental.pallas import tpu as pltpu
from jax.sharding import PartitionSpec as P

ITERS = 3
LANE = 128
GROUP = 32
BOTH = ("row", "col")
HIGH = lax.Precision.HIGHEST
NT = (((1,), (1,)), ((), ()))
NN = (((1,), (0,)), ((), ()))
SMEM = pl.BlockSpec(memory_space=pltpu.SMEM)
VMEM = pl.BlockSpec(memory_space=pltpu.VMEM)


def kernel_call(kernel, name, out, ins, scratch=()):
    return pl.pallas_call(
        kernel,
        name=name,
        out_shape=out,
        in_specs=ins,
        out_specs=jax.tree.map(lambda _: VMEM, out),
        scratch_shapes=scratch,
        compiler_params=pltpu.CompilerParams(vmem_limit_bytes=16 << 20),
    )


def f32(*shape):
    return jax.ShapeDtypeStruct(shape, jnp.float32)


def line(t, vecs, part):
    return pl.ds(t * vecs * 3 + part, vecs, stride=3)


def keep(split, slot, values):
    vecs = values.shape[0]
    high = values.astype(jnp.bfloat16)
    split[slot, 0:vecs, :] = high
    split[slot, vecs : 2 * vecs, :] = (values - high.astype(jnp.float32)).astype(jnp.bfloat16)


def multiply(index_ref, tiles_ref, split, total, direct, mirror):
    seg_tiles = total.shape[0] // 3
    vecs = total.shape[1]
    slots = tiles_ref.shape[0]
    count = index_ref[2 * slots]
    size = GROUP if slots % GROUP == 0 else slots
    total[...] = jnp.zeros_like(total)

    def group(g, carry):
        parts = []
        for j in range(size):
            slot = g * size + j
            row = index_ref[slot]
            col = index_ref[slots + slot] + seg_tiles
            tile = tiles_ref[slot]
            live = slot < count
            for wanted, taken, place, dims in ((direct, col, row, NT), (mirror, row, col, NN)):
                if wanted:
                    part = lax.dot_general(split[taken], tile, dims, preferred_element_type=jnp.float32)
                    parts.append((place, jnp.where(live, part[:vecs] + part[vecs:], 0.0)))
        for place, part in parts:
            total[place] += part
        return carry

    lax.fori_loop(0, (count + (size - 1)) // size, group, 0)


def first_mirror(index_ref, tiles_ref, seg_ref, out_ref, split, total):
    seg_tiles = total.shape[0] // 3
    for t in range(seg_tiles):
        keep(split, t, seg_ref[:, t * LANE : (t + 1) * LANE])
    multiply(index_ref, tiles_ref, split, total, False, True)
    out_ref[...] = total[seg_tiles : 3 * seg_tiles]


def first_direct(index_ref, tiles_ref, block_ref, mirrored_ref, out_ref, split, total):
    seg_tiles, vecs = total.shape[0] // 3, total.shape[1]
    for t in range(2 * seg_tiles):
        keep(split, seg_tiles + t, block_ref[t // 2, :, (t % 2) * LANE : (t % 2 + 1) * LANE])
    multiply(index_ref, tiles_ref, split, total, True, False)
    for t in range(seg_tiles):
        out_ref[line(t, vecs, 0), :] = total[t]
        for half in range(2):
            out_ref[line(t, vecs, 1 + half), :] = mirrored_ref[half * seg_tiles + t]


def multiply_all(index_ref, tiles_ref, all_ref, split, total):
    seg_tiles, vecs = total.shape[0] // 3, total.shape[1]
    for t in range(seg_tiles):
        for part in range(3):
            keep(split, part * seg_tiles + t, all_ref[line(t, vecs, part), :])
    multiply(index_ref, tiles_ref, split, total, True, True)


def multiply_next(index_ref, tiles_ref, all_ref, out_ref, split, total):
    seg_tiles, vecs = total.shape[0] // 3, total.shape[1]
    multiply_all(index_ref, tiles_ref, all_ref, split, total)
    for t in range(seg_tiles):
        for part in range(3):
            out_ref[line(t, vecs, part), :] = total[part * seg_tiles + t]


def multiply_last(index_ref, tiles_ref, all_ref, direct_ref, mirror_ref, split, total):
    multiply_all(index_ref, tiles_ref, all_ref, split, total)
    for refs, base in ((direct_ref, 0), (mirror_ref, total.shape[0] // 3)):
        for t in range(2 * refs.shape[0]):
            refs[t // 2, :, (t % 2) * LANE : (t % 2 + 1) * LANE] = total[base + t]


def add_up(rows, cols, got_ref, sums):
    for r in range(rows):
        half = r % 2
        sums[r // 2 : r // 2 + 1, half * LANE : (half + 1) * LANE] = jnp.sum(
            got_ref[line(r, cols, 0), :], axis=0, keepdims=True
        )
    for half in range(2):
        mirror = got_ref[line(0, cols, 1 + half), :]
        for r in range(1, rows):
            mirror = mirror + got_ref[line(r, cols, 1 + half), :]
        lanes = slice(half * LANE, (half + 1) * LANE)
        sums[:, lanes] = sums[:, lanes] + mirror


def sum_and_deal(rows, cols, got_ref, out_ref, sums):
    add_up(rows, cols, got_ref, sums)
    for r in range(rows):
        half = r % 2
        out_ref[line(r, cols, 0), :] = jnp.broadcast_to(
            sums[r // 2 : r // 2 + 1, half * LANE : (half + 1) * LANE], (cols, LANE)
        )
        for half in range(2):
            out_ref[line(r, cols, 1 + half), :] = sums[:, half * LANE : (half + 1) * LANE]


def gram(zero_ref, one_ref, two_ref, three_ref, gram_ref):
    vecs = three_ref.shape[0]
    basis = [zero_ref[...], one_ref[...], two_ref[...], three_ref[...]]
    parts = []
    for j in range(ITERS + 1):
        others = jnp.concatenate(basis[j : j + 2], axis=0)
        parts.append(
            lax.dot_general(basis[j], others, NT, precision=HIGH, preferred_element_type=jnp.float32)
        )
    parts.append(jnp.zeros((vecs, LANE - (2 * ITERS + 1) * vecs), jnp.float32))
    gram_ref[...] = jnp.concatenate(parts, axis=1)


def finish(states, last_ref, turn_ref, start_ref, one_ref, two_ref, eigen_ref, ritz_ref):
    vecs = eigen_ref.shape[0]

    def mul(a, b, dims=NN):
        full = jnp.concatenate([b, jnp.zeros((LANE - b.shape[0], b.shape[1]), jnp.float32)], axis=0)
        return lax.dot_general(a, full, dims, precision=HIGH, preferred_element_type=jnp.float32)

    moments = last_ref[0, 2]
    for c in range(1, last_ref.shape[0]):
        moments = moments + last_ref[c, 2]
    moments = moments * (1.0 / states)
    hankel = jnp.concatenate(
        [moments] + [pltpu.roll(moments, LANE - j * vecs, 1) for j in range(1, ITERS)], axis=0
    )
    eye = lax.broadcasted_iota(jnp.int32, (vecs, LANE), 0) == lax.broadcasted_iota(jnp.int32, (vecs, LANE), 1)
    iterate = eye.astype(jnp.float32)
    search = None
    for i in range(ITERS):
        keep_turn, step, past = (turn_ref[i, j] for j in range(3))
        weighted = mul(iterate, hankel) if i else moments
        own = mul(weighted, iterate, NT)
        theta = mul(pltpu.roll(weighted, LANE - vecs, 1), iterate, NT)
        images = mul(pltpu.roll(weighted, LANE - 2 * vecs, 1), iterate, NT)
        terms = jnp.where(eye, images, 0.0) - 2.0 * theta * theta + theta * mul(own, theta)
        spread = jnp.maximum(jnp.sum(terms, axis=0, keepdims=True), 0.0)
        scaled = step / jnp.sqrt(spread + 1e-06)
        residual = pltpu.roll(iterate, vecs, 1) - mul(theta, iterate)
        moved = mul(scaled, residual)
        if search is not None:
            moved = moved - mul(-past, search)
        iterate = moved - mul(-keep_turn, iterate)
        search = moved
    ritz_ref[...] = theta[:, :vecs]
    used = (ITERS + 1) * vecs
    terms = []
    rest = iterate[:, :used]
    for _ in range(3):
        terms.append(rest.astype(jnp.bfloat16))
        rest = rest - terms[-1].astype(jnp.float32)
    factors = jnp.concatenate(terms, axis=0)
    for t in range(eigen_ref.shape[1] // LANE):
        lanes = slice(t * LANE, (t + 1) * LANE)
        basis = [start_ref[:, lanes], one_ref[line(t, vecs, 0), :], two_ref[line(t, vecs, 0), :], last_ref[t // 2, t % 2]]
        basis = jnp.concatenate(basis, axis=0)
        high = basis.astype(jnp.bfloat16)
        low = (basis - high.astype(jnp.float32)).astype(jnp.bfloat16)
        large = lax.dot_general(factors, high, NN, preferred_element_type=jnp.float32)
        small = lax.dot_general(factors[: 2 * vecs], low, NN, preferred_element_type=jnp.float32)
        small = small[:vecs] + small[vecs:] + large[2 * vecs :]
        eigen_ref[:, lanes] = large[:vecs] + (large[vecs : 2 * vecs] + small)


def body(tiles, tile_row, tile_col, tile_counts, start, rotation):
    tiles = tiles.reshape(tiles.shape[2:])
    slots = tiles.shape[0]
    vecs, seg_rows = start.shape
    rows = lax.axis_size("row")
    cols = lax.axis_size("col")
    seg_tiles = seg_rows // LANE
    pair = 2 * LANE
    index = jnp.concatenate([tile_row.reshape(slots), tile_col.reshape(slots), tile_counts.reshape(1)])
    own_col = lax.axis_index("col")
    dealt = f32(rows * cols * 3, LANE)
    work = [
        pltpu.VMEM((3 * seg_tiles, 2 * vecs, LANE), jnp.bfloat16),
        pltpu.VMEM((3 * seg_tiles, vecs, LANE), jnp.float32),
    ]
    sums = [pltpu.VMEM((cols, pair), jnp.float32)]
    corner = []
    for r in range(rows):
        for c in range(cols):
            corner.append((r * cols + c, ((r % 2) * cols + c) * cols + r // 2))

    def swap(x):
        moved = lax.all_to_all(x.reshape(rows * cols, 3 * LANE), BOTH, 0, 0)
        return moved.reshape(rows * cols * 3, LANE)

    own_row = lax.axis_index("row")
    pairs = seg_tiles // 2
    size = 2 * vecs * 3

    def own_block_piece(x):
        x = lax.dynamic_slice_in_dim(x, place, size, 0).reshape(2, vecs, 3, LANE)
        x = jnp.where(low, x[:, :, 1], x[:, :, 2])
        return jnp.concatenate([x[0], x[1]], axis=1)

    def to_all(x, axis):
        count = lax.axis_size(axis)
        return lax.all_to_all(jnp.broadcast_to(x, (count,) + x.shape), axis, 0, 0)

    own_start = lax.dynamic_slice_in_dim(start, own_col * pair, pair, 1)
    piece = lax.ppermute(own_start, BOTH, corner)
    place = (own_row % pairs * size).astype(jnp.uint32)
    index, piece, place, low = lax.optimization_barrier((index, piece, place, own_row < pairs))
    block = to_all(piece, "row")
    mirrored = kernel_call(
        first_mirror, "first_mirror", f32(2 * seg_tiles, vecs, LANE), [SMEM] + [VMEM] * 2, work
    )(index, tiles, start)
    sent = kernel_call(first_direct, "first_direct", dealt, [SMEM] + [VMEM] * 3, work)(
        index, tiles, block, mirrored
    )
    images = []
    for i in range(ITERS - 1):
        given = kernel_call(
            functools.partial(sum_and_deal, rows, cols), "sum_and_deal", dealt, [VMEM], sums
        )(swap(sent))
        images.append(swap(given))
        if i < ITERS - 2:
            sent = kernel_call(multiply_next, "multiply_next", dealt, [SMEM] + [VMEM] * 2, work)(
                index, tiles, images[-1]
            )
    direct, mirror = kernel_call(
        multiply_last, "multiply_last", (f32(cols, vecs, pair), f32(rows, vecs, pair)), [SMEM] + [VMEM] * 2, work
    )(index, tiles, images[-1])

    direct = jnp.sum(lax.all_to_all(direct, "col", 0, 0), axis=0)
    direct, mirror, *kept = lax.optimization_barrier((direct, mirror, *images))
    direct = lax.ppermute(direct, BOTH, corner)
    last = jnp.sum(lax.all_to_all(mirror, "row", 0, 0), axis=0) + direct
    own = [own_block_piece(image) for image in kept]
    grams = kernel_call(gram, "gram", f32(vecs, LANE), [VMEM] * 4)(piece, *own, last)
    last = lax.ppermute(last, BOTH, [(to, at) for at, to in corner])
    grams = jnp.sum(to_all(grams, "row"), axis=0)
    last = to_all(jnp.stack([last[:, :LANE], last[:, LANE:], grams]), "col")
    turned = jnp.pad(jnp.swapaxes(rotation, 2, 3), ((0, 0),) * 3 + ((0, LANE - vecs),))
    return kernel_call(
        functools.partial(finish, seg_rows * rows), "finish", (f32(vecs, seg_rows), f32(vecs, vecs)), [VMEM] * 5
    )(last, turned, start, *images)


def solution(mesh):
    return jax.shard_map(
        body,
        mesh=mesh,
        in_specs=(
            P("row", "col", None, None, None),
            P("row", "col", None),
            P("row", "col", None),
            P("row", "col"),
            P(None, "row"),
            P(),
        ),
        out_specs=(P(None, "row"), P()),
        check_vma=False,
    )
```

```python
import functools

import jax
import jax.numpy as jnp
from jax import lax
from jax.experimental import pallas as pl
from jax.experimental.pallas import tpu as pltpu
from jax.sharding import PartitionSpec as P

ITERS = 3
LANE = 128
GROUP = 32
BOTH = ("row", "col")
HIGH = lax.Precision.HIGHEST
NT = (((1,), (1,)), ((), ()))
NN = (((1,), (0,)), ((), ()))
SMEM = pl.BlockSpec(memory_space=pltpu.SMEM)
VMEM = pl.BlockSpec(memory_space=pltpu.VMEM)


def kernel_call(kernel, name, out, ins, scratch=()):
    return pl.pallas_call(
        kernel,
        name=name,
        out_shape=out,
        in_specs=ins,
        out_specs=jax.tree.map(lambda _: VMEM, out),
        scratch_shapes=scratch,
        compiler_params=pltpu.CompilerParams(vmem_limit_bytes=16 << 20),
    )


def f32(*shape):
    return jax.ShapeDtypeStruct(shape, jnp.float32)


def line(t, vecs, part):
    return pl.ds(t * vecs * 3 + part, vecs, stride=3)


def keep(split, slot, values):
    vecs = values.shape[0]
    high = values.astype(jnp.bfloat16)
    split[slot, 0:vecs, :] = high
    split[slot, vecs : 2 * vecs, :] = (values - high.astype(jnp.float32)).astype(jnp.bfloat16)


def multiply(index_ref, tiles_ref, split, total, direct, mirror):
    seg_tiles = total.shape[0] // 3
    vecs = total.shape[1]
    slots = tiles_ref.shape[0]
    count = index_ref[2 * slots]
    size = GROUP if slots % GROUP == 0 else slots
    total[...] = jnp.zeros_like(total)

    def group(g, carry):
        parts = []
        for j in range(size):
            slot = g * size + j
            row = index_ref[slot]
            col = index_ref[slots + slot] + seg_tiles
            tile = tiles_ref[slot]
            live = slot < count
            for wanted, taken, place, dims in ((direct, col, row, NT), (mirror, row, col, NN)):
                if wanted:
                    part = lax.dot_general(split[taken], tile, dims, preferred_element_type=jnp.float32)
                    parts.append((place, jnp.where(live, part[:vecs] + part[vecs:], 0.0)))
        for place, part in parts:
            total[place] += part
        return carry

    lax.fori_loop(0, (count + (size - 1)) // size, group, 0)


def first_mirror(index_ref, tiles_ref, seg_ref, out_ref, split, total):
    seg_tiles = total.shape[0] // 3
    for t in range(seg_tiles):
        keep(split, t, seg_ref[:, t * LANE : (t + 1) * LANE])
    multiply(index_ref, tiles_ref, split, total, False, True)
    out_ref[...] = total[seg_tiles : 3 * seg_tiles]


def first_direct(index_ref, tiles_ref, block_ref, mirrored_ref, out_ref, split, total):
    seg_tiles, vecs = total.shape[0] // 3, total.shape[1]
    for t in range(2 * seg_tiles):
        keep(split, seg_tiles + t, block_ref[t // 2, :, (t % 2) * LANE : (t % 2 + 1) * LANE])
    multiply(index_ref, tiles_ref, split, total, True, False)
    for t in range(seg_tiles):
        out_ref[line(t, vecs, 0), :] = total[t]
        for half in range(2):
            out_ref[line(t, vecs, 1 + half), :] = mirrored_ref[half * seg_tiles + t]


def multiply_all(index_ref, tiles_ref, all_ref, split, total):
    seg_tiles, vecs = total.shape[0] // 3, total.shape[1]
    for t in range(seg_tiles):
        for part in range(3):
            keep(split, part * seg_tiles + t, all_ref[line(t, vecs, part), :])
    multiply(index_ref, tiles_ref, split, total, True, True)


def multiply_next(index_ref, tiles_ref, all_ref, out_ref, split, total):
    seg_tiles, vecs = total.shape[0] // 3, total.shape[1]
    multiply_all(index_ref, tiles_ref, all_ref, split, total)
    for t in range(seg_tiles):
        for part in range(3):
            out_ref[line(t, vecs, part), :] = total[part * seg_tiles + t]


def multiply_last(index_ref, tiles_ref, all_ref, direct_ref, mirror_ref, split, total):
    multiply_all(index_ref, tiles_ref, all_ref, split, total)
    for refs, base in ((direct_ref, 0), (mirror_ref, total.shape[0] // 3)):
        for t in range(2 * refs.shape[0]):
            refs[t // 2, :, (t % 2) * LANE : (t % 2 + 1) * LANE] = total[base + t]


def add_up(rows, cols, got_ref, sums):
    for r in range(rows):
        half = r % 2
        sums[r // 2 : r // 2 + 1, half * LANE : (half + 1) * LANE] = jnp.sum(
            got_ref[line(r, cols, 0), :], axis=0, keepdims=True
        )
    for half in range(2):
        mirror = got_ref[line(0, cols, 1 + half), :]
        for r in range(1, rows):
            mirror = mirror + got_ref[line(r, cols, 1 + half), :]
        lanes = slice(half * LANE, (half + 1) * LANE)
        sums[:, lanes] = sums[:, lanes] + mirror


def sum_and_deal(rows, cols, got_ref, out_ref, sums):
    add_up(rows, cols, got_ref, sums)
    for r in range(rows):
        half = r % 2
        out_ref[line(r, cols, 0), :] = jnp.broadcast_to(
            sums[r // 2 : r // 2 + 1, half * LANE : (half + 1) * LANE], (cols, LANE)
        )
        for half in range(2):
            out_ref[line(r, cols, 1 + half), :] = sums[:, half * LANE : (half + 1) * LANE]


def gram(zero_ref, one_ref, two_ref, three_ref, gram_ref):
    vecs = three_ref.shape[0]
    basis = [zero_ref[...], one_ref[...], two_ref[...], three_ref[...]]
    parts = []
    for j in range(ITERS + 1):
        others = jnp.concatenate(basis[j : j + 2], axis=0)
        parts.append(
            lax.dot_general(basis[j], others, NT, precision=HIGH, preferred_element_type=jnp.float32)
        )
    parts.append(jnp.zeros((vecs, LANE - (2 * ITERS + 1) * vecs), jnp.float32))
    gram_ref[...] = jnp.concatenate(parts, axis=1)


def finish(states, last_ref, turn_ref, start_ref, one_ref, two_ref, eigen_ref, ritz_ref):
    vecs = eigen_ref.shape[0]

    def mul(a, b, dims=NN):
        full = jnp.concatenate([b, jnp.zeros((LANE - b.shape[0], b.shape[1]), jnp.float32)], axis=0)
        return lax.dot_general(a, full, dims, precision=HIGH, preferred_element_type=jnp.float32)

    moments = last_ref[0, 2]
    for c in range(1, last_ref.shape[0]):
        moments = moments + last_ref[c, 2]
    moments = moments * (1.0 / states)
    hankel = jnp.concatenate(
        [moments] + [pltpu.roll(moments, LANE - j * vecs, 1) for j in range(1, ITERS)], axis=0
    )
    eye = lax.broadcasted_iota(jnp.int32, (vecs, LANE), 0) == lax.broadcasted_iota(jnp.int32, (vecs, LANE), 1)
    iterate = eye.astype(jnp.float32)
    search = None
    for i in range(ITERS):
        keep_turn, step, past = (turn_ref[i, j] for j in range(3))
        weighted = mul(iterate, hankel) if i else moments
        own = mul(weighted, iterate, NT)
        theta = mul(pltpu.roll(weighted, LANE - vecs, 1), iterate, NT)
        images = mul(pltpu.roll(weighted, LANE - 2 * vecs, 1), iterate, NT)
        terms = jnp.where(eye, images, 0.0) - 2.0 * theta * theta + theta * mul(own, theta)
        spread = jnp.maximum(jnp.sum(terms, axis=0, keepdims=True), 0.0)
        scaled = step / jnp.sqrt(spread + 1e-06)
        residual = pltpu.roll(iterate, vecs, 1) - mul(theta, iterate)
        moved = mul(scaled, residual)
        if search is not None:
            moved = moved - mul(-past, search)
        iterate = moved - mul(-keep_turn, iterate)
        search = moved
    ritz_ref[...] = theta[:, :vecs]
    used = (ITERS + 1) * vecs
    terms = []
    rest = iterate[:, :used]
    for _ in range(3):
        terms.append(rest.astype(jnp.bfloat16))
        rest = rest - terms[-1].astype(jnp.float32)
    factors = jnp.concatenate(terms, axis=0)
    for t in range(eigen_ref.shape[1] // LANE):
        lanes = slice(t * LANE, (t + 1) * LANE)
        basis = [start_ref[:, lanes], one_ref[line(t, vecs, 0), :], two_ref[line(t, vecs, 0), :], last_ref[t // 2, t % 2]]
        basis = jnp.concatenate(basis, axis=0)
        high = basis.astype(jnp.bfloat16)
        low = (basis - high.astype(jnp.float32)).astype(jnp.bfloat16)
        large = lax.dot_general(factors, high, NN, preferred_element_type=jnp.float32)
        small = lax.dot_general(factors[: 2 * vecs], low, NN, preferred_element_type=jnp.float32)
        small = small[:vecs] + small[vecs:] + large[2 * vecs :]
        eigen_ref[:, lanes] = large[:vecs] + (large[vecs : 2 * vecs] + small)


def body(tiles, tile_row, tile_col, tile_counts, start, rotation):
    tiles = tiles.reshape(tiles.shape[2:])
    slots = tiles.shape[0]
    vecs, seg_rows = start.shape
    rows = lax.axis_size("row")
    cols = lax.axis_size("col")
    seg_tiles = seg_rows // LANE
    pair = 2 * LANE
    index = jnp.concatenate([tile_row.reshape(slots), tile_col.reshape(slots), tile_counts.reshape(1)])
    own_col = lax.axis_index("col")
    dealt = f32(rows * cols * 3, LANE)
    work = [
        pltpu.VMEM((3 * seg_tiles, 2 * vecs, LANE), jnp.bfloat16),
        pltpu.VMEM((3 * seg_tiles, vecs, LANE), jnp.float32),
    ]
    sums = [pltpu.VMEM((cols, pair), jnp.float32)]
    corner = []
    for r in range(rows):
        for c in range(cols):
            corner.append((r * cols + c, ((r % 2) * cols + c) * cols + r // 2))

    def swap(x):
        moved = lax.all_to_all(x.reshape(rows * cols, 3 * LANE), BOTH, 0, 0)
        return moved.reshape(rows * cols * 3, LANE)

    own_row = lax.axis_index("row")
    pairs = seg_tiles // 2
    size = 2 * vecs * 3

    def own_block_piece(x):
        x = lax.dynamic_slice_in_dim(x, place, size, 0).reshape(2, vecs, 3, LANE)
        x = jnp.where(low, x[:, :, 1], x[:, :, 2])
        return jnp.concatenate([x[0], x[1]], axis=1)

    def to_all(x, axis):
        count = lax.axis_size(axis)
        return lax.all_to_all(jnp.broadcast_to(x, (count,) + x.shape), axis, 0, 0)

    own_start = lax.dynamic_slice_in_dim(start, own_col * pair, pair, 1)
    piece = lax.ppermute(own_start, BOTH, corner)
    mirrored = kernel_call(
        first_mirror, "first_mirror", f32(2 * seg_tiles, vecs, LANE), [SMEM] + [VMEM] * 2, work
    )(index, tiles, start)
    place = (own_row % pairs * size).astype(jnp.uint32)
    mirrored, piece, place, low = lax.optimization_barrier((mirrored, piece, place, own_row < pairs))
    block = to_all(piece, "row")
    sent = kernel_call(first_direct, "first_direct", dealt, [SMEM] + [VMEM] * 3, work)(
        index, tiles, block, mirrored
    )
    images = []
    for i in range(ITERS - 1):
        given = kernel_call(
            functools.partial(sum_and_deal, rows, cols), "sum_and_deal", dealt, [VMEM], sums
        )(swap(sent))
        images.append(swap(given))
        if i < ITERS - 2:
            sent = kernel_call(multiply_next, "multiply_next", dealt, [SMEM] + [VMEM] * 2, work)(
                index, tiles, images[-1]
            )
    direct, mirror = kernel_call(
        multiply_last, "multiply_last", (f32(cols, vecs, pair), f32(rows, vecs, pair)), [SMEM] + [VMEM] * 2, work
    )(index, tiles, images[-1])

    direct = jnp.sum(lax.all_to_all(direct, "col", 0, 0), axis=0)
    direct, mirror, *kept = lax.optimization_barrier((direct, mirror, *images))
    direct = lax.ppermute(direct, BOTH, corner)
    last = jnp.sum(lax.all_to_all(mirror, "row", 0, 0), axis=0) + direct
    own = [own_block_piece(image) for image in kept]
    grams = kernel_call(gram, "gram", f32(vecs, LANE), [VMEM] * 4)(piece, *own, last)
    last = lax.ppermute(last, BOTH, [(to, at) for at, to in corner])
    grams = jnp.sum(to_all(grams, "row"), axis=0)
    last = to_all(jnp.stack([last[:, :LANE], last[:, LANE:], grams]), "col")
    turned = jnp.pad(jnp.swapaxes(rotation, 2, 3), ((0, 0),) * 3 + ((0, LANE - vecs),))
    return kernel_call(
        functools.partial(finish, seg_rows * rows), "finish", (f32(vecs, seg_rows), f32(vecs, vecs)), [VMEM] * 5
    )(last, turned, start, *images)


def solution(mesh):
    return jax.shard_map(
        body,
        mesh=mesh,
        in_specs=(
            P("row", "col", None, None, None),
            P("row", "col", None),
            P("row", "col", None),
            P("row", "col"),
            P(None, "row"),
            P(),
        ),
        out_specs=(P(None, "row"), P()),
        check_vma=False,
    )
```

```python
import functools

import jax
import jax.numpy as jnp
from jax import lax
from jax.experimental import pallas as pl
from jax.experimental.pallas import tpu as pltpu
from jax.sharding import PartitionSpec as P

ITERS = 3
LANE = 128
GROUP = 32
BOTH = ("row", "col")
HIGH = lax.Precision.HIGHEST
NT = (((1,), (1,)), ((), ()))
NN = (((1,), (0,)), ((), ()))
SMEM = pl.BlockSpec(memory_space=pltpu.SMEM)
VMEM = pl.BlockSpec(memory_space=pltpu.VMEM)


def kernel_call(kernel, name, out, ins, scratch=()):
    return pl.pallas_call(
        kernel,
        name=name,
        out_shape=out,
        in_specs=ins,
        out_specs=jax.tree.map(lambda _: VMEM, out),
        scratch_shapes=scratch,
        compiler_params=pltpu.CompilerParams(vmem_limit_bytes=16 << 20),
    )


def f32(*shape):
    return jax.ShapeDtypeStruct(shape, jnp.float32)


def line(t, vecs, part):
    return pl.ds(t * vecs * 3 + part, vecs, stride=3)


def keep(split, slot, values):
    vecs = values.shape[0]
    high = values.astype(jnp.bfloat16)
    split[slot, 0:vecs, :] = high
    split[slot, vecs : 2 * vecs, :] = (values - high.astype(jnp.float32)).astype(jnp.bfloat16)


def multiply(index_ref, tiles_ref, split, total, direct, mirror):
    seg_tiles = total.shape[0] // 3
    vecs = total.shape[1]
    slots = tiles_ref.shape[0]
    count = index_ref[2 * slots]
    size = GROUP if slots % GROUP == 0 else slots
    total[...] = jnp.zeros_like(total)

    def group(g, carry):
        parts = []
        for j in range(size):
            slot = g * size + j
            row = index_ref[slot]
            col = index_ref[slots + slot] + seg_tiles
            tile = tiles_ref[slot]
            live = slot < count
            for wanted, taken, place, dims in ((direct, col, row, NT), (mirror, row, col, NN)):
                if wanted:
                    part = lax.dot_general(split[taken], tile, dims, preferred_element_type=jnp.float32)
                    parts.append((place, jnp.where(live, part[:vecs] + part[vecs:], 0.0)))
        for place, part in parts:
            total[place] += part
        return carry

    lax.fori_loop(0, (count + (size - 1)) // size, group, 0)


def first_mirror(index_ref, tiles_ref, seg_ref, out_ref, split, total):
    seg_tiles = total.shape[0] // 3
    for t in range(seg_tiles):
        keep(split, t, seg_ref[:, t * LANE : (t + 1) * LANE])
    multiply(index_ref, tiles_ref, split, total, False, True)
    out_ref[...] = total[seg_tiles : 3 * seg_tiles]


def first_direct(index_ref, tiles_ref, block_ref, mirrored_ref, out_ref, split, total):
    seg_tiles, vecs = total.shape[0] // 3, total.shape[1]
    for t in range(2 * seg_tiles):
        keep(split, seg_tiles + t, block_ref[t // 2, :, (t % 2) * LANE : (t % 2 + 1) * LANE])
    multiply(index_ref, tiles_ref, split, total, True, False)
    for t in range(seg_tiles):
        out_ref[line(t, vecs, 0), :] = total[t]
        for half in range(2):
            out_ref[line(t, vecs, 1 + half), :] = mirrored_ref[half * seg_tiles + t]


def multiply_all(index_ref, tiles_ref, all_ref, split, total):
    seg_tiles, vecs = total.shape[0] // 3, total.shape[1]
    for t in range(seg_tiles):
        for part in range(3):
            keep(split, part * seg_tiles + t, all_ref[line(t, vecs, part), :])
    multiply(index_ref, tiles_ref, split, total, True, True)


def multiply_next(index_ref, tiles_ref, all_ref, out_ref, split, total):
    seg_tiles, vecs = total.shape[0] // 3, total.shape[1]
    multiply_all(index_ref, tiles_ref, all_ref, split, total)
    for t in range(seg_tiles):
        for part in range(3):
            out_ref[line(t, vecs, part), :] = total[part * seg_tiles + t]


def multiply_last(index_ref, tiles_ref, all_ref, direct_ref, mirror_ref, split, total):
    multiply_all(index_ref, tiles_ref, all_ref, split, total)
    for refs, base in ((direct_ref, 0), (mirror_ref, total.shape[0] // 3)):
        for t in range(2 * refs.shape[0]):
            refs[t // 2, :, (t % 2) * LANE : (t % 2 + 1) * LANE] = total[base + t]


def add_up(rows, cols, got_ref, sums):
    for r in range(rows):
        half = r % 2
        sums[r // 2 : r // 2 + 1, half * LANE : (half + 1) * LANE] = jnp.sum(
            got_ref[line(r, cols, 0), :], axis=0, keepdims=True
        )
    for half in range(2):
        mirror = got_ref[line(0, cols, 1 + half), :]
        for r in range(1, rows):
            mirror = mirror + got_ref[line(r, cols, 1 + half), :]
        lanes = slice(half * LANE, (half + 1) * LANE)
        sums[:, lanes] = sums[:, lanes] + mirror


def sum_and_deal(rows, cols, got_ref, out_ref, sums):
    add_up(rows, cols, got_ref, sums)
    for r in range(rows):
        half = r % 2
        out_ref[line(r, cols, 0), :] = jnp.broadcast_to(
            sums[r // 2 : r // 2 + 1, half * LANE : (half + 1) * LANE], (cols, LANE)
        )
        for half in range(2):
            out_ref[line(r, cols, 1 + half), :] = sums[:, half * LANE : (half + 1) * LANE]


def gram(zero_ref, one_ref, two_ref, three_ref, gram_ref):
    vecs = three_ref.shape[0]
    basis = [zero_ref[...], one_ref[...], two_ref[...], three_ref[...]]
    parts = []
    for j in range(ITERS + 1):
        others = jnp.concatenate(basis[j : j + 2], axis=0)
        parts.append(
            lax.dot_general(basis[j], others, NT, precision=HIGH, preferred_element_type=jnp.float32)
        )
    parts.append(jnp.zeros((vecs, LANE - (2 * ITERS + 1) * vecs), jnp.float32))
    gram_ref[...] = jnp.concatenate(parts, axis=1)


def finish(states, last_ref, turn_ref, start_ref, one_ref, two_ref, eigen_ref, ritz_ref):
    vecs = eigen_ref.shape[0]

    def mul(a, b, dims=NN):
        full = jnp.concatenate([b, jnp.zeros((LANE - b.shape[0], b.shape[1]), jnp.float32)], axis=0)
        return lax.dot_general(a, full, dims, precision=HIGH, preferred_element_type=jnp.float32)

    moments = last_ref[0, 2]
    for c in range(1, last_ref.shape[0]):
        moments = moments + last_ref[c, 2]
    moments = moments * (1.0 / states)
    hankel = jnp.concatenate(
        [moments] + [pltpu.roll(moments, LANE - j * vecs, 1) for j in range(1, ITERS)], axis=0
    )
    eye = lax.broadcasted_iota(jnp.int32, (vecs, LANE), 0) == lax.broadcasted_iota(jnp.int32, (vecs, LANE), 1)
    iterate = eye.astype(jnp.float32)
    search = None
    for i in range(ITERS):
        keep_turn, step, past = (turn_ref[i, j] for j in range(3))
        weighted = mul(iterate, hankel) if i else moments
        own = mul(weighted, iterate, NT)
        theta = mul(pltpu.roll(weighted, LANE - vecs, 1), iterate, NT)
        images = mul(pltpu.roll(weighted, LANE - 2 * vecs, 1), iterate, NT)
        terms = jnp.where(eye, images, 0.0) - 2.0 * theta * theta + theta * mul(own, theta)
        spread = jnp.maximum(jnp.sum(terms, axis=0, keepdims=True), 0.0)
        scaled = step / jnp.sqrt(spread + 1e-06)
        residual = pltpu.roll(iterate, vecs, 1) - mul(theta, iterate)
        moved = mul(scaled, residual)
        if search is not None:
            moved = moved - mul(-past, search)
        iterate = moved - mul(-keep_turn, iterate)
        search = moved
    ritz_ref[...] = theta[:, :vecs]
    used = (ITERS + 1) * vecs
    terms = []
    rest = iterate[:, :used]
    for _ in range(3):
        terms.append(rest.astype(jnp.bfloat16))
        rest = rest - terms[-1].astype(jnp.float32)
    factors = jnp.concatenate(terms, axis=0)
    for t in range(eigen_ref.shape[1] // LANE):
        lanes = slice(t * LANE, (t + 1) * LANE)
        basis = [start_ref[:, lanes], one_ref[line(t, vecs, 0), :], two_ref[line(t, vecs, 0), :], last_ref[t // 2, t % 2]]
        basis = jnp.concatenate(basis, axis=0)
        high = basis.astype(jnp.bfloat16)
        low = (basis - high.astype(jnp.float32)).astype(jnp.bfloat16)
        large = lax.dot_general(factors, high, NN, preferred_element_type=jnp.float32)
        small = lax.dot_general(factors[: 2 * vecs], low, NN, preferred_element_type=jnp.float32)
        small = small[:vecs] + small[vecs:] + large[2 * vecs :]
        eigen_ref[:, lanes] = large[:vecs] + (large[vecs : 2 * vecs] + small)


def body(tiles, tile_row, tile_col, tile_counts, start, rotation):
    tiles = tiles.reshape(tiles.shape[2:])
    slots = tiles.shape[0]
    vecs, seg_rows = start.shape
    rows = lax.axis_size("row")
    cols = lax.axis_size("col")
    seg_tiles = seg_rows // LANE
    pair = 2 * LANE
    index = jnp.concatenate([tile_row.reshape(slots), tile_col.reshape(slots), tile_counts.reshape(1)])
    own_col = lax.axis_index("col")
    dealt = f32(rows * cols * 3, LANE)
    work = [
        pltpu.VMEM((3 * seg_tiles, 2 * vecs, LANE), jnp.bfloat16),
        pltpu.VMEM((3 * seg_tiles, vecs, LANE), jnp.float32),
    ]
    sums = [pltpu.VMEM((cols, pair), jnp.float32)]
    corner = []
    for r in range(rows):
        for c in range(cols):
            corner.append((r * cols + c, ((r % 2) * cols + c) * cols + r // 2))

    def swap(x):
        moved = lax.all_to_all(x.reshape(rows * cols, 3 * LANE), BOTH, 0, 0)
        return moved.reshape(rows * cols * 3, LANE)

    own_row = lax.axis_index("row")
    pairs = seg_tiles // 2
    size = 2 * vecs * 3

    def own_block_piece(x):
        x = lax.dynamic_slice_in_dim(x, place, size, 0).reshape(2, vecs, 3, LANE)
        x = jnp.where(low, x[:, :, 1], x[:, :, 2])
        return jnp.concatenate([x[0], x[1]], axis=1)

    def to_all(x, axis):
        count = lax.axis_size(axis)
        return lax.all_to_all(jnp.broadcast_to(x, (count,) + x.shape), axis, 0, 0)

    own_start = lax.dynamic_slice_in_dim(start, own_col * pair, pair, 1)
    piece = lax.ppermute(own_start, BOTH, corner)
    mirrored = kernel_call(
        first_mirror, "first_mirror", f32(2 * seg_tiles, vecs, LANE), [SMEM] + [VMEM] * 2, work
    )(index, tiles, start)
    place = (own_row % pairs * size).astype(jnp.uint32)
    mirrored, piece, place, low = lax.optimization_barrier((mirrored, piece, place, own_row < pairs))
    block = to_all(piece, "row")
    sent = kernel_call(first_direct, "first_direct", dealt, [SMEM] + [VMEM] * 3, work)(
        index, tiles, block, mirrored
    )
    images = []
    for i in range(ITERS - 1):
        given = kernel_call(
            functools.partial(sum_and_deal, rows, cols), "sum_and_deal", dealt, [VMEM], sums
        )(swap(sent))
        images.append(swap(given))
        if i < ITERS - 2:
            sent = kernel_call(multiply_next, "multiply_next", dealt, [SMEM] + [VMEM] * 2, work)(
                index, tiles, images[-1]
            )
    direct, mirror = kernel_call(
        multiply_last, "multiply_last", (f32(cols, vecs, pair), f32(rows, vecs, pair)), [SMEM] + [VMEM] * 2, work
    )(index, tiles, images[-1])

    direct = jnp.sum(lax.all_to_all(direct, "col", 0, 0), axis=0)
    direct, mirror, rotation, *kept = lax.optimization_barrier((direct, mirror, rotation, *images))
    turned = jnp.pad(jnp.swapaxes(rotation, 2, 3), ((0, 0),) * 3 + ((0, LANE - vecs),))
    direct = lax.ppermute(direct, BOTH, corner)
    last = jnp.sum(lax.all_to_all(mirror, "row", 0, 0), axis=0) + direct
    own = [own_block_piece(image) for image in kept]
    grams = kernel_call(gram, "gram", f32(vecs, LANE), [VMEM] * 4)(piece, *own, last)
    last = lax.ppermute(last, BOTH, [(to, at) for at, to in corner])
    grams = jnp.sum(to_all(grams, "row"), axis=0)
    last, turned = lax.optimization_barrier((jnp.stack([last[:, :LANE], last[:, LANE:], grams]), turned))
    last = to_all(last, "col")
    return kernel_call(
        functools.partial(finish, seg_rows * rows), "finish", (f32(vecs, seg_rows), f32(vecs, vecs)), [VMEM] * 5
    )(last, turned, start, *images)


def solution(mesh):
    return jax.shard_map(
        body,
        mesh=mesh,
        in_specs=(
            P("row", "col", None, None, None),
            P("row", "col", None),
            P("row", "col", None),
            P("row", "col"),
            P(None, "row"),
            P(),
        ),
        out_specs=(P(None, "row"), P()),
        check_vma=False,
    )
```

```python
import functools

import jax
import jax.numpy as jnp
from jax import lax
from jax.experimental import pallas as pl
from jax.experimental.pallas import tpu as pltpu
from jax.sharding import PartitionSpec as P

ITERS = 3
LANE = 128
GROUP = 32
BOTH = ("row", "col")
HIGH = lax.Precision.HIGHEST
NT = (((1,), (1,)), ((), ()))
NN = (((1,), (0,)), ((), ()))
SMEM = pl.BlockSpec(memory_space=pltpu.SMEM)
VMEM = pl.BlockSpec(memory_space=pltpu.VMEM)


def kernel_call(kernel, name, out, ins, scratch=()):
    return pl.pallas_call(
        kernel,
        name=name,
        out_shape=out,
        in_specs=ins,
        out_specs=jax.tree.map(lambda _: VMEM, out),
        scratch_shapes=scratch,
        compiler_params=pltpu.CompilerParams(vmem_limit_bytes=16 << 20),
    )


def f32(*shape):
    return jax.ShapeDtypeStruct(shape, jnp.float32)


def line(t, vecs, part):
    return pl.ds(t * vecs * 3 + part, vecs, stride=3)


def keep(split, slot, values):
    vecs = values.shape[0]
    high = values.astype(jnp.bfloat16)
    split[slot, 0:vecs, :] = high
    split[slot, vecs : 2 * vecs, :] = (values - high.astype(jnp.float32)).astype(jnp.bfloat16)


def multiply(index_ref, tiles_ref, split, total, direct, mirror):
    seg_tiles = total.shape[0] // 3
    vecs = total.shape[1]
    slots = tiles_ref.shape[0]
    count = index_ref[2 * slots]
    size = GROUP if slots % GROUP == 0 else slots
    total[...] = jnp.zeros_like(total)

    def group(g, carry):
        parts = []
        for j in range(size):
            slot = g * size + j
            row = index_ref[slot]
            col = index_ref[slots + slot] + seg_tiles
            tile = tiles_ref[slot]
            live = slot < count
            for wanted, taken, place, dims in ((direct, col, row, NT), (mirror, row, col, NN)):
                if wanted:
                    part = lax.dot_general(split[taken], tile, dims, preferred_element_type=jnp.float32)
                    parts.append((place, jnp.where(live, part[:vecs] + part[vecs:], 0.0)))
        for place, part in parts:
            total[place] += part
        return carry

    lax.fori_loop(0, (count + (size - 1)) // size, group, 0)


def first_mirror(index_ref, tiles_ref, seg_ref, out_ref, split, total):
    seg_tiles = total.shape[0] // 3
    for t in range(seg_tiles):
        keep(split, t, seg_ref[:, t * LANE : (t + 1) * LANE])
    multiply(index_ref, tiles_ref, split, total, False, True)
    out_ref[...] = total[seg_tiles : 3 * seg_tiles]


def first_direct(index_ref, tiles_ref, block_ref, mirrored_ref, out_ref, split, total):
    seg_tiles, vecs = total.shape[0] // 3, total.shape[1]
    for t in range(2 * seg_tiles):
        keep(split, seg_tiles + t, block_ref[t // 2, :, (t % 2) * LANE : (t % 2 + 1) * LANE])
    multiply(index_ref, tiles_ref, split, total, True, False)
    for t in range(seg_tiles):
        out_ref[line(t, vecs, 0), :] = total[t]
        for half in range(2):
            out_ref[line(t, vecs, 1 + half), :] = mirrored_ref[half * seg_tiles + t]


def multiply_all(index_ref, tiles_ref, all_ref, split, total):
    seg_tiles, vecs = total.shape[0] // 3, total.shape[1]
    for t in range(seg_tiles):
        for part in range(3):
            keep(split, part * seg_tiles + t, all_ref[line(t, vecs, part), :])
    multiply(index_ref, tiles_ref, split, total, True, True)


def multiply_next(index_ref, tiles_ref, all_ref, out_ref, split, total):
    seg_tiles, vecs = total.shape[0] // 3, total.shape[1]
    multiply_all(index_ref, tiles_ref, all_ref, split, total)
    for t in range(seg_tiles):
        for part in range(3):
            out_ref[line(t, vecs, part), :] = total[part * seg_tiles + t]


def multiply_last(index_ref, tiles_ref, all_ref, direct_ref, mirror_ref, split, total):
    multiply_all(index_ref, tiles_ref, all_ref, split, total)
    for refs, base in ((direct_ref, 0), (mirror_ref, total.shape[0] // 3)):
        for t in range(2 * refs.shape[0]):
            refs[t // 2, :, (t % 2) * LANE : (t % 2 + 1) * LANE] = total[base + t]


def add_up(rows, cols, got_ref, sums):
    for r in range(rows):
        half = r % 2
        sums[r // 2 : r // 2 + 1, half * LANE : (half + 1) * LANE] = jnp.sum(
            got_ref[line(r, cols, 0), :], axis=0, keepdims=True
        )
    for half in range(2):
        mirror = got_ref[line(0, cols, 1 + half), :]
        for r in range(1, rows):
            mirror = mirror + got_ref[line(r, cols, 1 + half), :]
        lanes = slice(half * LANE, (half + 1) * LANE)
        sums[:, lanes] = sums[:, lanes] + mirror


def sum_and_deal(rows, cols, got_ref, out_ref, sums):
    add_up(rows, cols, got_ref, sums)
    for r in range(rows):
        half = r % 2
        out_ref[line(r, cols, 0), :] = jnp.broadcast_to(
            sums[r // 2 : r // 2 + 1, half * LANE : (half + 1) * LANE], (cols, LANE)
        )
        for half in range(2):
            out_ref[line(r, cols, 1 + half), :] = sums[:, half * LANE : (half + 1) * LANE]


def gram(zero_ref, one_ref, two_ref, direct_ref, parts_ref, three_ref, gram_ref):
    vecs = direct_ref.shape[0]
    three = parts_ref[0]
    for r in range(1, parts_ref.shape[0]):
        three = three + parts_ref[r]
    three = three + direct_ref[...]
    three_ref[...] = three
    basis = [zero_ref[...], one_ref[...], two_ref[...], three]
    parts = []
    for j in range(ITERS + 1):
        others = jnp.concatenate(basis[j : j + 2], axis=0)
        parts.append(
            lax.dot_general(basis[j], others, NT, precision=HIGH, preferred_element_type=jnp.float32)
        )
    parts.append(jnp.zeros((vecs, LANE - (2 * ITERS + 1) * vecs), jnp.float32))
    grams = jnp.concatenate(parts, axis=1)
    for r in range(gram_ref.shape[0]):
        gram_ref[r] = grams


def finish(states, last_ref, turn_ref, start_ref, one_ref, two_ref, eigen_ref, ritz_ref):
    vecs = eigen_ref.shape[0]

    def mul(a, b, dims=NN):
        full = jnp.concatenate([b, jnp.zeros((LANE - b.shape[0], b.shape[1]), jnp.float32)], axis=0)
        return lax.dot_general(a, full, dims, precision=HIGH, preferred_element_type=jnp.float32)

    moments = last_ref[0, 2]
    for c in range(1, last_ref.shape[0]):
        moments = moments + last_ref[c, 2]
    moments = moments * (1.0 / states)
    hankel = jnp.concatenate(
        [moments] + [pltpu.roll(moments, LANE - j * vecs, 1) for j in range(1, ITERS)], axis=0
    )
    eye = lax.broadcasted_iota(jnp.int32, (vecs, LANE), 0) == lax.broadcasted_iota(jnp.int32, (vecs, LANE), 1)
    iterate = eye.astype(jnp.float32)
    search = None
    for i in range(ITERS):
        keep_turn, step, past = (turn_ref[i, j] for j in range(3))
        weighted = mul(iterate, hankel) if i else moments
        own = mul(weighted, iterate, NT)
        theta = mul(pltpu.roll(weighted, LANE - vecs, 1), iterate, NT)
        images = mul(pltpu.roll(weighted, LANE - 2 * vecs, 1), iterate, NT)
        terms = jnp.where(eye, images, 0.0) - 2.0 * theta * theta + theta * mul(own, theta)
        spread = jnp.maximum(jnp.sum(terms, axis=0, keepdims=True), 0.0)
        scaled = step / jnp.sqrt(spread + 1e-06)
        residual = pltpu.roll(iterate, vecs, 1) - mul(theta, iterate)
        moved = mul(scaled, residual)
        if search is not None:
            moved = moved - mul(-past, search)
        iterate = moved - mul(-keep_turn, iterate)
        search = moved
    ritz_ref[...] = theta[:, :vecs]
    used = (ITERS + 1) * vecs
    terms = []
    rest = iterate[:, :used]
    for _ in range(3):
        terms.append(rest.astype(jnp.bfloat16))
        rest = rest - terms[-1].astype(jnp.float32)
    factors = jnp.concatenate(terms, axis=0)
    for t in range(eigen_ref.shape[1] // LANE):
        lanes = slice(t * LANE, (t + 1) * LANE)
        basis = [start_ref[:, lanes], one_ref[line(t, vecs, 0), :], two_ref[line(t, vecs, 0), :], last_ref[t // 2, t % 2]]
        basis = jnp.concatenate(basis, axis=0)
        high = basis.astype(jnp.bfloat16)
        low = (basis - high.astype(jnp.float32)).astype(jnp.bfloat16)
        large = lax.dot_general(factors, high, NN, preferred_element_type=jnp.float32)
        small = lax.dot_general(factors[: 2 * vecs], low, NN, preferred_element_type=jnp.float32)
        small = small[:vecs] + small[vecs:] + large[2 * vecs :]
        eigen_ref[:, lanes] = large[:vecs] + (large[vecs : 2 * vecs] + small)


def body(tiles, tile_row, tile_col, tile_counts, start, rotation):
    tiles = tiles.reshape(tiles.shape[2:])
    slots = tiles.shape[0]
    vecs, seg_rows = start.shape
    rows = lax.axis_size("row")
    cols = lax.axis_size("col")
    seg_tiles = seg_rows // LANE
    pair = 2 * LANE
    index = jnp.concatenate([tile_row.reshape(slots), tile_col.reshape(slots), tile_counts.reshape(1)])
    own_col = lax.axis_index("col")
    dealt = f32(rows * cols * 3, LANE)
    work = [
        pltpu.VMEM((3 * seg_tiles, 2 * vecs, LANE), jnp.bfloat16),
        pltpu.VMEM((3 * seg_tiles, vecs, LANE), jnp.float32),
    ]
    sums = [pltpu.VMEM((cols, pair), jnp.float32)]
    corner = []
    for r in range(rows):
        for c in range(cols):
            corner.append((r * cols + c, ((r % 2) * cols + c) * cols + r // 2))

    def swap(x):
        moved = lax.all_to_all(x.reshape(rows * cols, 3 * LANE), BOTH, 0, 0)
        return moved.reshape(rows * cols * 3, LANE)

    own_row = lax.axis_index("row")
    pairs = seg_tiles // 2
    size = 2 * vecs * 3

    def own_block_piece(x):
        x = lax.dynamic_slice_in_dim(x, place, size, 0).reshape(2, vecs, 3, LANE)
        x = jnp.where(low, x[:, :, 1], x[:, :, 2])
        return jnp.concatenate([x[0], x[1]], axis=1)

    def to_all(x, axis):
        count = lax.axis_size(axis)
        return lax.all_to_all(jnp.broadcast_to(x, (count,) + x.shape), axis, 0, 0)

    own_start = lax.dynamic_slice_in_dim(start, own_col * pair, pair, 1)
    piece = lax.ppermute(own_start, BOTH, corner)
    mirrored = kernel_call(
        first_mirror, "first_mirror", f32(2 * seg_tiles, vecs, LANE), [SMEM] + [VMEM] * 2, work
    )(index, tiles, start)
    place = (own_row % pairs * size).astype(jnp.uint32)
    mirrored, piece, place, low = lax.optimization_barrier((mirrored, piece, place, own_row < pairs))
    block = to_all(piece, "row")
    sent = kernel_call(first_direct, "first_direct", dealt, [SMEM] + [VMEM] * 3, work)(
        index, tiles, block, mirrored
    )
    images = []
    for i in range(ITERS - 1):
        given = kernel_call(
            functools.partial(sum_and_deal, rows, cols), "sum_and_deal", dealt, [VMEM], sums
        )(swap(sent))
        images.append(swap(given))
        if i < ITERS - 2:
            sent = kernel_call(multiply_next, "multiply_next", dealt, [SMEM] + [VMEM] * 2, work)(
                index, tiles, images[-1]
            )
    direct, mirror = kernel_call(
        multiply_last, "multiply_last", (f32(cols, vecs, pair), f32(rows, vecs, pair)), [SMEM] + [VMEM] * 2, work
    )(index, tiles, images[-1])

    direct = jnp.sum(lax.all_to_all(direct, "col", 0, 0), axis=0)
    direct, mirror, rotation, *kept = lax.optimization_barrier((direct, mirror, rotation, *images))
    turned = jnp.pad(jnp.swapaxes(rotation, 2, 3), ((0, 0),) * 3 + ((0, LANE - vecs),))
    direct = lax.ppermute(direct, BOTH, corner)
    parts = lax.all_to_all(mirror, "row", 0, 0)
    own = [own_block_piece(image) for image in kept]
    last, grams = kernel_call(gram, "gram", (f32(vecs, pair), f32(rows, vecs, LANE)), [VMEM] * 5)(
        piece, *own, direct, parts
    )
    last = lax.ppermute(last, BOTH, [(to, at) for at, to in corner])
    grams = jnp.sum(lax.all_to_all(grams, "row", 0, 0), axis=0)
    last, turned = lax.optimization_barrier((jnp.stack([last[:, :LANE], last[:, LANE:], grams]), turned))
    last = to_all(last, "col")
    return kernel_call(
        functools.partial(finish, seg_rows * rows), "finish", (f32(vecs, seg_rows), f32(vecs, vecs)), [VMEM] * 5
    )(last, turned, start, *images)


def solution(mesh):
    return jax.shard_map(
        body,
        mesh=mesh,
        in_specs=(
            P("row", "col", None, None, None),
            P("row", "col", None),
            P("row", "col", None),
            P("row", "col"),
            P(None, "row"),
            P(),
        ),
        out_specs=(P(None, "row"), P()),
        check_vma=False,
    )
```
